256 devices in a mesh: dp: 8 (over y, core), vocab: 32 (over z, x).
Axes of the slice: x: 4, y: 4, z: 8, core: 2. Of those that a mesh axis runs over, the one named last changes fastest.
Arguments:
- hidden: bfloat16 [512, 4096], P('dp'), may hold values from -26 to 26
- head_weight: bfloat16 [4096, 151552], P(None, ('dp', 'vocab')), may hold values from -0.3 to 0.3
- teacher_ids: int32 [512, 64], P('dp'), may hold values from 0 to 151551
- teacher_logits: bfloat16 [512, 64], P('dp'), may hold values from -30 to 405
- labels: int32 [512], P('dp'), may hold values from 0 to 151551
- store_ids: int32 [4096, 64], P(('dp', 'vocab')), may hold values from 0 to 151551
- store_logits: bfloat16 [4096, 64], P(('dp', 'vocab')), may hold values from -18 to 18
- owner: int32 [4096, 1], P(('dp', 'vocab')), may hold values from 0 to 7; in each aligned block of 16 rows (0 to 15, 16 to 31, ...) at most 4 rows name the same one
Outputs:
- grad_head: bfloat16 [4096, 151552], P(None, ('dp', 'vocab'))
- grad_hidden: bfloat16 [512, 4096], P('dp', 'vocab')
- token_loss: float32 [512], P('dp')
- next_ids: int32 [8192, 64], P(('dp', 'vocab'))
- next_logits: bfloat16 [8192, 64], P(('dp', 'vocab'))
The draws below stay inside these ranges and needn't reach their ends.
Inputs may be any that keep to these rules, and one draw needn't show every extreme that they name: Of the 16 rows of one store shard, at most 4 have the same owner, and some shard has exactly 4 rows for one owner.
All inputs are finite; a program needn't handle non-finite values.
Results may differ from the reference program's by a relative error of at most 0.0034.
Values may be sent and summed in bfloat16 or wider, within the bound.
No kernel may reach another device: no remote copies, remote signals or barrier semaphores. Data moves between devices by JAX's collectives and lax.ppermute only.
A program may use at most 64 MiB of HBM per device.

```python
import math
import jax
import jax.numpy as jnp
import numpy as np
from jax import lax

D = 4096
VOCAB = 151552
TOPK = 64
SHARD_ROWS = 16
TOKENS = 512
CAP = 4
STORE_ROWS = 4096
N_DP = 8
N_VOCAB = 32


def column_block(key, block_index, col_width):
    values = jax.random.normal(jax.random.fold_in(key, 5000 + block_index), (D, col_width), jnp.float32)
    return jnp.clip(values, -6.0, 6.0) * (3.0 / math.sqrt(D))


def draw_head_weight(key, part):
    col_width = math.gcd(VOCAB, 4096)
    blocks = lax.map(lambda block_index: column_block(key, block_index, col_width), jnp.arange(VOCAB // col_width, dtype=jnp.int32))
    return jnp.transpose(blocks, (1, 0, 2)).reshape(D, VOCAB).astype(jnp.bfloat16)


def draw_hidden(key, part):
    key = jax.random.fold_in(key, 21)
    key_drawn = jax.random.fold_in(key, 1)
    values = jnp.clip(jax.random.normal(key_drawn, (TOKENS, D), jnp.float32), -6.0, 6.0)
    return values.astype(jnp.bfloat16)


def draw_teacher_logits(key, part):
    key = jax.random.fold_in(key, 33)
    key_low = jax.random.fold_in(key, 1)
    key_values = jax.random.fold_in(key, 2)
    offsets = jax.random.uniform(key_low, (TOKENS, 1), jnp.float32, 5.0, 25.0)
    values = offsets + 3.0 * jnp.clip(jax.random.normal(key_values, (TOKENS, TOPK), jnp.float32), -6.0, 6.0)
    return values.astype(jnp.bfloat16)


def with_ends(array, rng, least, high):
    shape = array.shape
    index_at = [jax.random.randint(jax.random.fold_in(rng, axis), (), 0, shape[axis]) for axis in range(len(shape))]
    array = array.at[tuple(index_at)].set(least)
    longest = shape.index(max(shape))
    index_at[longest] = (index_at[longest] + 1) % shape[longest]
    return array.at[tuple(index_at)].set(high)


def steps_of(rng, shape, shards, smallest, top_value):
    level, own = 1.0, jax.random.fold_in(rng, 6)
    for axis_at, blocks in shards:
        draws = jnp.exp(jax.random.uniform(jax.random.fold_in(own, axis_at), (blocks,), jnp.float32, smallest / len(shards), top_value / len(shards)))
        level = level * jnp.repeat(draws, shape[axis_at] // blocks).reshape([-1 if axis == axis_at else 1 for axis in range(len(shape))])
    return level


def ranked_wide(own_key, shape, count, slope):
    portions = [min(1 << octave, count + 1 - (1 << octave)) * (1 << 20) // math.isqrt((1 << octave) ** slope) + 1 for octave in range((count + 1).bit_length()) if 1 << octave <= count]
    spread = 1 + sum(portions) // (1 << 30)
    listing = np.cumsum(np.array([max(1, weight // spread) for weight in portions]))
    lot = jax.random.randint(jax.random.fold_in(own_key, 1), shape, 0, int(listing[len(portions) - 1]))
    start = jnp.left_shift(1, jnp.searchsorted(jnp.asarray(listing, jnp.int32), lot, side="right").astype(jnp.int32))
    standing = start - 1 + jax.random.randint(jax.random.fold_in(own_key, 4), shape, 0, 1 << 30) % jnp.minimum(start, count + 1 - start)
    return jax.random.permutation(jax.random.fold_in(own_key, 2), count)[standing].astype(jnp.int32)


def assign_block(rng, own, number, rows, number_of, top, limit, lean):
    ranking = jax.random.permutation(rng, number_of)
    crowded, ordinary = shares(number_of, rows * top, limit, lean, True), shares(number_of, rows * top, limit, lean, False)
    places = jnp.arange(number_of)

    def named(tallies, turn):
        used = int((tallies > 0).sum())
        fixed = max(1, used // 4)
        passed = fixed + (places - fixed + turn * (used - fixed)) % max(1, number_of - fixed)
        return jnp.zeros((number_of,), jnp.int32).at[ranking[jnp.where(places < fixed, places, passed)]].set(jnp.asarray(tallies, jnp.int32))

    tallies = jnp.where(number % 4 == 0, named(crowded, number // 4), named(ordinary, number - number // 4 - 1))
    mixed = jax.random.permutation(jax.random.fold_in(own, 3), number_of)
    donor, receiver = mixed[0:number_of // 2 * 2:2], mixed[1:number_of // 2 * 2:2]
    slack = jnp.minimum(tallies[donor] - 1, limit - tallies[receiver]) // 2
    slack = jnp.where((donor == ranking[0]) | (receiver == ranking[0]) | (tallies[receiver] == 0), 0, jnp.maximum(slack, 0))
    passed = jax.random.randint(jax.random.fold_in(own, 4), (number_of // 2,), 0, 1 << 20) % (slack + 1)
    tallies = tallies.at[donor].add(-passed).at[receiver].add(passed)
    members = jnp.searchsorted(jnp.cumsum(tallies), jnp.arange(rows * top), side="right").astype(jnp.int32)
    grid = members.reshape(top, rows).T
    grid = grid[jax.random.permutation(jax.random.fold_in(own, 1), rows)]
    turn = jax.random.randint(jax.random.fold_in(own, 2), (rows, 1), 0, top)
    return jnp.take_along_axis(grid, (jnp.arange(top)[None, :] + turn) % top, axis=1)


def shares(number_of, total, limit, lean, full):
    loads = [(1 << 20) // math.isqrt(grade ** lean) + 1 for grade in range(1, number_of + 1)]
    largest = limit if full else min(limit, max(-(-total // number_of), total * loads[0] // sum(loads)))
    least = 1 if total - largest >= number_of - 1 else 0
    holding, surplus = [largest] + [least] * (number_of - 1), total - largest - least * (number_of - 1)
    while surplus > 0:
        candidates = [i for i in range(1, number_of) if holding[i] < largest] or [i for i in range(1, number_of) if holding[i] < limit]
        pool, left = sum([loads[i] for i in candidates]), surplus
        for i in candidates:
            addition = min(limit - holding[i], max(1, left * loads[i] // pool), surplus)
            holding[i] = holding[i] + addition
            surplus = surplus - addition
    return np.array(holding)


def noise(stream_key, dims, scale, reach, cuts=(), kind=jnp.bfloat16):
    entries = scale * jax.random.normal(stream_key, dims, jnp.float32)
    if cuts:
        entries = entries * steps_of(stream_key, dims, cuts, -0.22, 0.18)
    return jnp.clip(entries, -reach, reach).astype(kind)


def setup_inputs(seed: int = 0) -> dict:
    key_list = jax.random.split(jax.random.key(seed), 9)
    hidden = draw_hidden(jax.random.fold_in(key_list[8], 71), 0)
    head_weight = draw_head_weight(jax.random.fold_in(key_list[8], 71), 0)
    teacher_ids = with_ends(ranked_wide(key_list[2], (TOKENS, TOPK), VOCAB, 1), jax.random.fold_in(key_list[2], 3), 0, VOCAB - 1).astype(jnp.int32)
    teacher_logits = draw_teacher_logits(jax.random.fold_in(key_list[8], 71), 0)
    labels = with_ends(jax.random.randint(key_list[4], (TOKENS,), 0, VOCAB), jax.random.fold_in(key_list[4], 1), 0, VOCAB - 1).astype(jnp.int32)
    store_ids = with_ends(ranked_wide(key_list[5], (STORE_ROWS, TOPK), VOCAB, 1), jax.random.fold_in(key_list[5], 3), 0, VOCAB - 1).astype(jnp.int32)
    store_logits = noise(key_list[6], (STORE_ROWS, TOPK), 3.0, 18.0, ((0, 256),))
    owner_keys = jax.random.split(jax.random.fold_in(key_list[7], 1), STORE_ROWS // SHARD_ROWS)
    owner_turns = jax.random.permutation(jax.random.fold_in(key_list[7], 3), STORE_ROWS // SHARD_ROWS)
    owner = jax.vmap(lambda own, number: assign_block(jax.random.fold_in(key_list[7], 2), own, number, SHARD_ROWS, N_DP, 1, CAP, 2))(owner_keys, owner_turns).reshape((STORE_ROWS, 1))
    return dict(hidden=hidden, head_weight=head_weight, teacher_ids=teacher_ids, teacher_logits=teacher_logits, labels=labels, store_ids=store_ids, store_logits=store_logits, owner=owner)


mixing = 0.5
loss_scale = 64.0


def reference(hidden, head_weight, teacher_ids, teacher_logits, labels, store_ids, store_logits, owner):
    col_width = math.gcd(VOCAB, 4096)
    col_blocks = VOCAB // col_width
    tokens_all = hidden.shape[0]
    hidden_wide = hidden.astype(jnp.float32)

    def block_logits(block_index):
        weight_cols = lax.dynamic_slice_in_dim(head_weight, block_index * col_width, col_width, 1).astype(jnp.float32)
        return jnp.dot(hidden_wide, weight_cols, precision=lax.Precision.HIGHEST)

    stacked = lax.map(block_logits, jnp.arange(col_blocks, dtype=jnp.int32))
    logits = jnp.transpose(stacked, (1, 0, 2)).reshape(tokens_all, VOCAB)
    row_peak = jnp.max(logits, axis=1)
    row_total = jnp.sum(jnp.exp(logits - row_peak[:, None]), axis=1)
    log_norm = row_peak + jnp.log(row_total)
    teacher_raw = teacher_logits.astype(jnp.float32)
    shifted = teacher_raw - jnp.max(teacher_raw, axis=1, keepdims=True)
    teacher_logp = shifted - jnp.log(jnp.sum(jnp.exp(shifted), axis=1, keepdims=True))
    teacher_prob = jnp.exp(teacher_logp)
    picked = jnp.take_along_axis(logits, teacher_ids, axis=1)
    label_logit = jnp.take_along_axis(logits, labels[:, None], axis=1)[:, 0]
    cross_term = mixing * jnp.sum(teacher_prob * picked, axis=1) + (1.0 - mixing) * label_logit
    token_loss = mixing * jnp.sum(teacher_prob * teacher_logp, axis=1) + log_norm - cross_term
    row_index = jnp.arange(tokens_all, dtype=jnp.int32)
    target = jnp.zeros((tokens_all, VOCAB), jnp.float32)
    target = target.at[row_index[:, None], teacher_ids].add(mixing * teacher_prob)
    target = target.at[row_index, labels].add(1.0 - mixing)
    grad_logits = (loss_scale * (jnp.exp(logits - log_norm[:, None]) - target)).astype(jnp.bfloat16)

    def block_grads(carry, block_index):
        weight_cols = lax.dynamic_slice_in_dim(head_weight, block_index * col_width, col_width, 1).astype(jnp.float32)
        grad_cols = lax.dynamic_slice_in_dim(grad_logits, block_index * col_width, col_width, 1).astype(jnp.float32)
        head_block = jnp.dot(hidden_wide.T, grad_cols, precision=lax.Precision.HIGHEST).astype(jnp.bfloat16)
        carry = carry + jnp.dot(grad_cols, weight_cols.T, precision=lax.Precision.HIGHEST)
        return carry, head_block

    hidden_sum, head_blocks = lax.scan(block_grads, jnp.zeros((tokens_all, D), jnp.float32), jnp.arange(col_blocks, dtype=jnp.int32))
    grad_head = jnp.transpose(head_blocks, (1, 0, 2)).reshape(D, VOCAB)
    grad_hidden = hidden_sum.astype(jnp.bfloat16)

    shard_count = owner.shape[0] // SHARD_ROWS
    owner_dev = owner[:, 0].reshape(shard_count, SHARD_ROWS)
    position = jnp.arange(SHARD_ROWS, dtype=jnp.int32)
    same_owner = (owner_dev[:, :, None] == owner_dev[:, None, :]) & (position[None, None, :] < position[None, :, None])
    slot_index = jnp.sum(same_owner.astype(jnp.int32), axis=2)
    shard_index = jnp.arange(shard_count, dtype=jnp.int32)[:, None]
    flat_index = (((owner_dev * N_VOCAB + shard_index % N_VOCAB) * N_DP + shard_index // N_VOCAB) * CAP + slot_index).reshape(-1)
    out_rows = N_DP * N_VOCAB * N_DP * CAP
    next_ids = jnp.full((out_rows, TOPK), -1, jnp.int32).at[flat_index].set(store_ids)
    next_logits = jnp.zeros((out_rows, TOPK), jnp.bfloat16).at[flat_index].set(store_logits)
    return (grad_head, grad_hidden, token_loss, next_ids, next_logits)
```

```python
import functools

import jax
import jax.numpy as jnp
from jax import lax
from jax.experimental import pallas as pl
from jax.experimental.pallas import tpu as pltpu
from jax.sharding import PartitionSpec as P

mixing = 0.5
loss_scale = 64.0
f32 = jnp.float32
bf16 = jnp.bfloat16
NY, NC, NZ, NX = 4, 2, 8, 4
AXES = ("y", "c", "z", "x")
ROWS = 64
TOK = NY * ROWS
D = 4096
COLS = 592
TOPK = 64
CAP = 4
HALF = ROWS // 2
VMEM = 48 * 1024 * 1024


def index_of(y, c, z, x):
    return (((y % NY) * NC + c % NC) * NZ + z % NZ) * NX + x % NX


def send(value, dy=0, dc=0, dz=0, dx=0):
    pairs = [
        (index_of(y, c, z, x), index_of(y + dy, c + dc, z + dz, x + dx))
        for y in range(NY)
        for c in range(NC)
        for z in range(NZ)
        for x in range(NX)
    ]
    return lax.ppermute(value, AXES, pairs)


def params():
    return pltpu.CompilerParams(vmem_limit_bytes=VMEM)


def whole():
    return pl.BlockSpec(memory_space=pltpu.VMEM)


def cost(flops, size):
    return pl.CostEstimate(flops=flops, bytes_accessed=size, transcendentals=0)


def target_kernel(start_ref, ids_ref, scores_ref, label_ref, own_ref, par_ref, tk_ref, prob_ref):
    scores = scores_ref[...]
    shifted = scores - jnp.max(scores, axis=0, keepdims=True)
    logp = shifted - jnp.log(jnp.sum(jnp.exp(shifted), axis=0, keepdims=True))
    prob = jnp.exp(logp)
    tk_ref[...] = mixing * jnp.sum(prob * logp, axis=0, keepdims=True)
    prob_ref[...] = mixing * prob
    label = label_ref[...]
    step = 16

    def rows(i, carry):
        first = pl.multiple_of(i * step, step)
        iota = lax.broadcasted_iota(jnp.int32, (step, TOK), 0) + first
        cols_own = iota + start_ref[0]
        cols_par = iota + start_ref[1]
        own = jnp.where(cols_own == label, 1.0 - mixing, 0.0)
        par = jnp.where(cols_par == label, 1.0 - mixing, 0.0)
        for k in range(TOPK):
            ids = ids_ref[pl.ds(k, 1), :]
            p = prob_ref[pl.ds(k, 1), :]
            own = own + jnp.where(cols_own == ids, p, 0.0)
            par = par + jnp.where(cols_par == ids, p, 0.0)
        own_ref[pl.ds(first, step), :] = own
        par_ref[pl.ds(first, step), :] = par
        return carry

    lax.fori_loop(0, COLS // step, rows, 0)


def target_of(start, ids, scores, label):
    return pl.pallas_call(
        target_kernel,
        out_shape=(
            jax.ShapeDtypeStruct((COLS, TOK), f32),
            jax.ShapeDtypeStruct((COLS, TOK), f32),
            jax.ShapeDtypeStruct((1, TOK), f32),
        ),
        in_specs=[pl.BlockSpec(memory_space=pltpu.SMEM), whole(), whole(), whole()],
        out_specs=(whole(), whole(), whole()),
        scratch_shapes=[pltpu.VMEM((TOPK, TOK), f32)],
        compiler_params=params(),
        cost_estimate=cost(8_000_000_000, 1_400_000),
        name="target",
    )(start, ids, scores, label)


def logits_kernel(h0, h1, h2, h3, wo, wp, to, tp, lo, lp, stats, hid):
    step = pl.program_id(0)
    h = jnp.concatenate([h0[...], h1[...], h2[...], h3[...]], axis=0)
    hid[...] = h
    dims = (((1,), (1,)), ((), ()))
    a = lax.dot_general(wo[...], h, dims, preferred_element_type=f32)
    b = lax.dot_general(wp[...], h, dims, preferred_element_type=f32)

    @pl.when(step == 0)
    def _():
        lo[...] = a
        lp[...] = b

    @pl.when(step > 0)
    def _():
        lo[...] += a
        lp[...] += b

    @pl.when(step == pl.num_programs(0) - 1)
    def _():
        own, par = lo[...], lp[...]
        peak = jnp.maximum(
            jnp.max(own, axis=0, keepdims=True), jnp.max(par, axis=0, keepdims=True)
        )
        total = jnp.sum(jnp.exp(own - peak), axis=0, keepdims=True) + jnp.sum(
            jnp.exp(par - peak), axis=0, keepdims=True
        )
        cross = jnp.sum(own * to[...], axis=0, keepdims=True) + jnp.sum(
            par * tp[...], axis=0, keepdims=True
        )
        stats[...] = jnp.concatenate([peak, total, cross, jnp.zeros((5, TOK), f32)], axis=0)


def logits_of(blocks, wo, wp, to, tp):
    steps = 8
    k = D // steps
    fixed = lambda shape: pl.BlockSpec(shape, lambda i: (0, 0))
    return pl.pallas_call(
        logits_kernel,
        grid=(steps,),
        out_shape=(
            jax.ShapeDtypeStruct((COLS, TOK), f32),
            jax.ShapeDtypeStruct((COLS, TOK), f32),
            jax.ShapeDtypeStruct((8, TOK), f32),
            jax.ShapeDtypeStruct((TOK, D), bf16),
        ),
        in_specs=[pl.BlockSpec((ROWS, k), lambda i: (0, i))] * 4
        + [pl.BlockSpec((COLS, k), lambda i: (0, i))] * 2
        + [fixed((COLS, TOK))] * 2,
        out_specs=(
            fixed((COLS, TOK)),
            fixed((COLS, TOK)),
            fixed((8, TOK)),
            pl.BlockSpec((TOK, k), lambda i: (0, i)),
        ),
        compiler_params=params(),
        cost_estimate=cost(2 * TOK * D * COLS * 2, 14_000_000),
        name="logits",
    )(*blocks, wo, wp, to, tp)


def merge(parts):
    peak = parts[0][0:1]
    for p in parts[1:]:
        peak = jnp.maximum(peak, p[0:1])
    total = sum(p[1:2] * jnp.exp(p[0:1] - peak) for p in parts)
    cross = sum(p[2:3] for p in parts)
    return peak, total, cross


def merge_kernel(shifts, *refs):
    parts = []
    for ref, shift in zip(refs[:-1], shifts):
        part = ref[...]
        if shift:
            part = pltpu.roll(part, TOK - shift * ROWS, 1)
        parts.append(part)
    peak, total, cross = merge(parts)
    refs[-1][...] = jnp.concatenate([peak, total, cross, jnp.zeros((5, TOK), f32)], axis=0)


def merged(parts, shifts):
    return pl.pallas_call(
        functools.partial(merge_kernel, shifts),
        out_shape=jax.ShapeDtypeStruct((8, TOK), f32),
        in_specs=[whole()] * len(parts),
        out_specs=whole(),
        compiler_params=params(),
        name="merge",
    )(*parts)


def final_kernel(tk, *refs):
    peak, total, cross = merge([ref[...] for ref in refs[:-1]])
    norm = peak + jnp.log(total)
    refs[-1][...] = jnp.concatenate(
        [norm, tk[...] + norm - cross, jnp.zeros((6, TOK), f32)], axis=0
    )


def final_norm(tk, parts):
    return pl.pallas_call(
        final_kernel,
        out_shape=jax.ShapeDtypeStruct((8, TOK), f32),
        in_specs=[whole()] * (len(parts) + 1),
        out_specs=whole(),
        compiler_params=params(),
        name="norm",
    )(tk, *parts)


def grads_kernel(place, lo, lp, to, tp, norm, wo, wp, go_ref, gp_ref, *rest):
    outs_a, outs_b = rest[0:4], rest[4:8]
    g_own, g_par = rest[8], rest[9]

    @pl.when(pl.program_id(0) == 0)
    def _():
        n = norm[0:1, :]
        own = (loss_scale * (jnp.exp(lo[...] - n) - to[...])).astype(bf16)
        par = (loss_scale * (jnp.exp(lp[...] - n) - tp[...])).astype(bf16)
        go_ref[...] = own
        gp_ref[...] = par
        g_own[...] = own.T
        g_par[...] = par.T

    x = place[1]

    def features(ref):
        return jnp.concatenate(
            [ref[:, pl.ds(pl.multiple_of(((x + d) % NX) * 128, 128), 128)] for d in range(NX)],
            axis=1,
        )

    out = jnp.dot(g_own[...], features(wo), preferred_element_type=f32)
    out = out + jnp.dot(g_par[...], features(wp), preferred_element_type=f32)
    for d in range(NX):
        for r in range(NY):
            piece = out[r * ROWS : (r + 1) * ROWS, d * 128 : (d + 1) * 128]
            outs_a[d][r] = piece[:HALF].astype(outs_a[d].dtype)
            outs_b[r][d] = piece[HALF:].astype(outs_b[r].dtype)


def grads_of(place, lo, lp, to, tp, norm, wo, wp):
    fixed = lambda shape: pl.BlockSpec(shape, lambda e, place: (0,) * len(shape))
    wide = pl.BlockSpec((COLS, NX * 128), lambda e, place: (0, (place[0] + e) % NZ))
    piece = pl.BlockSpec((4, HALF, 128), lambda e, place: (0, 0, e))
    out = [jax.ShapeDtypeStruct((4, HALF, NZ * 128), t) for t in (f32, bf16, bf16, bf16)]
    return pl.pallas_call(
        grads_kernel,
        grid_spec=pltpu.PrefetchScalarGridSpec(
            num_scalar_prefetch=1,
            grid=(NZ,),
            in_specs=[fixed((COLS, TOK))] * 4 + [fixed((8, TOK)), wide, wide],
            out_specs=[fixed((COLS, TOK))] * 2 + [piece] * 8,
            scratch_shapes=[pltpu.VMEM((TOK, COLS), bf16)] * 2,
        ),
        out_shape=[jax.ShapeDtypeStruct((COLS, TOK), bf16)] * 2 + out + out,
        compiler_params=params(),
        cost_estimate=cost(2 * TOK * D * COLS * 2, 16_000_000),
        name="grads",
    )(place, lo, lp, to, tp, norm, wo, wp)


def sum_first_kernel(*refs):
    for half in range(2):
        ins, outs = refs[4 * half : 4 * half + 4], refs[8 + 4 * half : 12 + 4 * half]
        for r in range(4):
            total = ins[0][r]
            for ref in ins[1:]:
                total = total + ref[r].astype(f32)
            outs[r][...] = total


def sum_first(a, b):
    out = jax.ShapeDtypeStruct((HALF, NZ * 128), f32)
    res = pl.pallas_call(
        sum_first_kernel,
        out_shape=[out] * 8,
        in_specs=[whole()] * 8,
        out_specs=[whole()] * 8,
        compiler_params=params(),
        name="sum_first",
    )(*a, *b)
    return res[:4], res[4:]


def sum_second_kernel(*refs):
    ins_a, ins_b, outs = refs[0:4], refs[4:8], refs[8:]
    for e in range(NZ):
        at = slice(e * 128, (e + 1) * 128)
        outs[e][:HALF] = ins_a[0][:, at] + ins_a[1][:, at] + ins_a[2][:, at] + ins_a[3][:, at]
        outs[e][HALF:] = ins_b[0][:, at] + ins_b[1][:, at] + ins_b[2][:, at] + ins_b[3][:, at]


def sum_second(a, b):
    return pl.pallas_call(
        sum_second_kernel,
        out_shape=[jax.ShapeDtypeStruct((ROWS, 128), f32)] * NZ,
        in_specs=[whole()] * 8,
        out_specs=[whole()] * NZ,
        compiler_params=params(),
        name="sum_second",
    )(*a, *b)


def head_kernel(g0, g1, h0, h1, out):
    total = jnp.dot(g0[...], h0[...], preferred_element_type=f32)
    total = total + jnp.dot(g1[...], h1[...], preferred_element_type=f32)
    out[...] = total.astype(bf16)


def head_grad(g0, g1, h0, h1):
    width = 512
    return pl.pallas_call(
        head_kernel,
        grid=(D // width,),
        out_shape=jax.ShapeDtypeStruct((COLS, D), bf16),
        in_specs=[pl.BlockSpec((COLS, TOK), lambda i: (0, 0))] * 2
        + [pl.BlockSpec((TOK, width), lambda i: (0, i))] * 2,
        out_specs=pl.BlockSpec((COLS, width), lambda i: (0, i)),
        compiler_params=params(),
        cost_estimate=cost(4 * TOK * D * COLS, 10_000_000),
        name="head_grad",
    )(g0, g1, h0, h1)


def store_blocks(store_ids, store_logits, owner, y, c):
    rows = owner.shape[0]
    named = owner[:, 0]
    position = jnp.arange(rows, dtype=jnp.int32)
    before = (named[:, None] == named[None, :]) & (position[None, :] < position[:, None])
    slot = jnp.sum(before.astype(jnp.int32), axis=1)
    block = (((named // NC) - y) % NY) * NC + (named % NC + c) % NC
    slots = jnp.arange(NY * NC * CAP, dtype=jnp.int32)
    placed = slots[:, None] == (block * CAP + slot)[None, :]
    filled = jnp.any(placed, axis=1)
    values = jnp.concatenate([store_ids.astype(f32), store_logits.astype(f32)], axis=1)
    sums = jnp.sum(jnp.where(placed[:, :, None], values[None, :, :], 0.0), axis=1)
    empty = jnp.where(jnp.arange(2 * TOPK) < TOPK, -1.0, 0.0)
    return jnp.where(filled[:, None], sums, empty[None, :])


def body(hidden, head_weight, teacher_ids, teacher_logits, labels, store_ids, store_logits, owner):
    y, c, z, x = (lax.axis_index(name).astype(jnp.int32) for name in AXES)
    w_own = jnp.transpose(head_weight)
    w_par = send(w_own, dc=1)

    stored = store_blocks(store_ids, store_logits, owner, y, c)
    teacher = jnp.concatenate(
        [teacher_ids.astype(f32).T, teacher_logits.astype(f32).T], axis=1
    )
    label_row = jnp.pad(labels.astype(f32)[None, :], ((0, 7), (0, 2 * ROWS - ROWS)))
    packs = []
    for d in range(NY):
        pack = jnp.concatenate([teacher, label_row, stored[d * 8 : d * 8 + 8]], axis=0)
        packs.append(send(pack, dy=d) if d else pack)
    ids_rows = jnp.concatenate([p[:TOPK, :ROWS] for p in packs], axis=1).astype(jnp.int32)
    scores = jnp.concatenate([p[:TOPK, ROWS:] for p in packs], axis=1)
    label_rows = jnp.concatenate([p[TOPK : TOPK + 1, :ROWS] for p in packs], axis=1).astype(
        jnp.int32
    )
    start = jnp.stack(
        [index_of(y, c, z, x) * COLS, index_of(y, c + 1, z, x) * COLS]
    ).astype(jnp.int32)

    blocks = [send(hidden, dy=d) if d else hidden for d in range(NY)]

    to, tp, tk = target_of(start, ids_rows, scores, label_rows)
    lo, lp, stats, hid = logits_of(blocks, w_own, w_par, to, tp)

    parts = [stats] + [send(stats, dx=d) for d in range(1, NX)]
    stats = merged(parts, (0,) * NX)
    parts = [stats] + [send(stats, dy=-d) for d in range(1, NY)]
    stats = merged(parts, tuple(range(NY)))
    parts = [stats] + [send(stats, dz=d) for d in range(1, NZ)]
    norm = final_norm(tk, parts)
    token_loss = norm[1, :ROWS]

    place = jnp.stack([z, x])
    go, gp, *terms = grads_of(place, lo, lp, to, tp, norm, w_own, w_par)
    a, b = terms[0:4], terms[4:8]
    a = [a[0]] + [send(a[d], dx=d) for d in range(1, NX)]
    b = [b[0]] + [send(b[d], dy=-d) for d in range(1, NY)]
    a, b = sum_first(a, b)
    a = [a[0]] + [send(a[d], dy=-d) for d in range(1, NY)]
    b = [b[0]] + [send(b[d], dx=d) for d in range(1, NX)]
    last = sum_second(a, b)
    grad_hidden = last[0]
    for e in range(1, NZ):
        grad_hidden = grad_hidden + send(last[e], dz=e)
    grad_hidden = grad_hidden.astype(bf16)

    hid_par = send(hid, dc=1)
    g_other = send(gp, dc=1)
    grad_head = jnp.transpose(head_grad(go, g_other, hid, hid_par))

    kept = jnp.stack([p[TOPK + 8 : TOPK + 8 + CAP] for p in packs])
    passed = send(jnp.stack([p[TOPK + 8 + CAP :] for p in packs]), dc=1)
    by_core = jnp.where(
        c == 0, jnp.stack([kept, passed], axis=1), jnp.stack([passed, kept], axis=1)
    )
    source = jnp.arange(NY, dtype=jnp.int32)
    pick = source[None, :] == ((y - source) % NY)[:, None]
    ordered = jnp.sum(jnp.where(pick[:, :, None, None, None], by_core[None], 0.0), axis=1)
    ordered = ordered.reshape(NY * NC * CAP, 2 * TOPK)
    next_ids = ordered[:, :TOPK].astype(jnp.int32)
    next_logits = ordered[:, TOPK:].astype(bf16)
    return (grad_head, grad_hidden, token_loss, next_ids, next_logits)


def solution(mesh):
    fine = jax.sharding.Mesh(mesh.devices.reshape(NY, NC, NZ, NX), AXES)
    dp, vocab, both = ("y", "c"), ("z", "x"), AXES
    return jax.shard_map(
        body,
        mesh=fine,
        in_specs=(
            P(dp, None),
            P(None, both),
            P(dp, None),
            P(dp, None),
            P(dp),
            P(both, None),
            P(both, None),
            P(both, None),
        ),
        out_specs=(
            P(None, both),
            P(dp, vocab),
            P(dp),
            P(both, None),
            P(both, None),
        ),
        check_vma=False,
    )
```

```python
import functools

import jax
import jax.numpy as jnp
from jax import lax
from jax.experimental import pallas as pl
from jax.experimental.pallas import tpu as pltpu
from jax.sharding import PartitionSpec as P

mixing = 0.5
loss_scale = 64.0
f32 = jnp.float32
bf16 = jnp.bfloat16
NY, NC, NZ, NX = 4, 2, 8, 4
AXES = ("y", "c", "z", "x")
ROWS = 64
TOK = NY * ROWS
D = 4096
COLS = 592
TOPK = 64
CAP = 4
HALF = ROWS // 2
VMEM = 48 * 1024 * 1024
ZSTEP = 4
TARGET_COST = 1_000_000


def index_of(y, c, z, x):
    return (((y % NY) * NC + c % NC) * NZ + z % NZ) * NX + x % NX


def send(value, dy=0, dc=0, dz=0, dx=0):
    pairs = [
        (index_of(y, c, z, x), index_of(y + dy, c + dc, z + dz, x + dx))
        for y in range(NY)
        for c in range(NC)
        for z in range(NZ)
        for x in range(NX)
    ]
    return lax.ppermute(value, AXES, pairs)


def params(size=VMEM):
    return pltpu.CompilerParams(vmem_limit_bytes=size)


def whole():
    return pl.BlockSpec(memory_space=pltpu.VMEM)


def cost(flops, size):
    return pl.CostEstimate(flops=flops, bytes_accessed=size, transcendentals=0)


def pack_kernel(place, owner, ids, scores, label, store_ids, store_logits, *outs):
    y, c = place[2], place[3]
    entries = jnp.concatenate([ids[...].astype(f32), scores[...].astype(f32)], axis=1).T
    teacher = jnp.concatenate([entries[:TOPK], entries[TOPK:]], axis=1)
    label_rows = jnp.concatenate([label[...].astype(f32), jnp.zeros((1, ROWS), f32)], axis=1)
    label_rows = jnp.concatenate([label_rows, jnp.zeros((7, 2 * ROWS), f32)], axis=0)
    lane = lax.broadcasted_iota(jnp.int32, (NC * CAP, 2 * TOPK), 1)
    empty = jnp.where(lane < TOPK, -1.0, 0.0)
    for out in outs:
        out[0:TOPK, :] = teacher
        out[TOPK : TOPK + 8, :] = label_rows
        out[TOPK + 8 : TOPK + 16, :] = empty
    rows = store_ids.shape[0]
    values = jnp.concatenate(
        [store_ids[...].astype(f32), store_logits[...].astype(f32)], axis=1
    )
    for j in range(rows):
        named = owner[j]
        slot = jnp.int32(0)
        for i in range(j):
            slot = slot + (owner[i] == named).astype(jnp.int32)
        ahead = ((named >> 1) + NY - y) & (NY - 1)
        row = TOPK + 8 + ((named + c) & 1) * CAP + slot
        for d in range(NY):

            @pl.when(ahead == d)
            def _(out=outs[d], row=row, j=j):
                out[pl.ds(row, 1), :] = values[j : j + 1, :]


def packs_of(place, owner, ids, scores, label, store_ids, store_logits):
    smem = pl.BlockSpec(memory_space=pltpu.SMEM)
    return pl.pallas_call(
        pack_kernel,
        out_shape=[jax.ShapeDtypeStruct((TOPK + 16, 2 * TOPK), f32)] * NY,
        in_specs=[smem, smem] + [whole()] * 5,
        out_specs=[whole()] * NY,
        compiler_params=params(60 * 1024 * 1024),
        name="pack",
    )(place, owner, ids, scores, label, store_ids, store_logits)


def target_kernel(start_ref, p0, p1, p2, p3, own_ref, par_ref, tk_ref, kept_ref, pass_ref, ids_ref, prob_ref):
    packs = (p0, p1, p2, p3)
    ids_ref[...] = jnp.concatenate([p[0:TOPK, :ROWS] for p in packs], axis=1).astype(jnp.int32)
    scores = jnp.concatenate([p[0:TOPK, ROWS:] for p in packs], axis=1)
    label = jnp.concatenate([p[TOPK : TOPK + 1, :ROWS] for p in packs], axis=1).astype(jnp.int32)
    for d, p in enumerate(packs):
        kept_ref[d * CAP : (d + 1) * CAP, :] = p[TOPK + 8 : TOPK + 8 + CAP, :]
        pass_ref[d * CAP : (d + 1) * CAP, :] = p[TOPK + 8 + CAP : TOPK + 16, :]
    shifted = scores - jnp.max(scores, axis=0, keepdims=True)
    logp = shifted - jnp.log(jnp.sum(jnp.exp(shifted), axis=0, keepdims=True))
    prob = jnp.exp(logp)
    tk_ref[...] = mixing * jnp.sum(prob * logp, axis=0, keepdims=True)
    prob_ref[...] = mixing * prob
    step = 16

    def rows(i, carry):
        first = pl.multiple_of(i * step, step)
        iota = lax.broadcasted_iota(jnp.int32, (step, TOK), 0) + first
        cols_own = iota + start_ref[0]
        cols_par = iota + start_ref[1]
        own = jnp.where(cols_own == label, 1.0 - mixing, 0.0)
        par = jnp.where(cols_par == label, 1.0 - mixing, 0.0)
        for k in range(TOPK):
            ids = ids_ref[pl.ds(k, 1), :]
            p = prob_ref[pl.ds(k, 1), :]
            own = own + jnp.where(cols_own == ids, p, 0.0)
            par = par + jnp.where(cols_par == ids, p, 0.0)
        own_ref[pl.ds(first, step), :] = own
        par_ref[pl.ds(first, step), :] = par
        return carry

    lax.fori_loop(0, COLS // step, rows, 0)


def target_of(start, packs):
    stored = jax.ShapeDtypeStruct((NY * CAP, 2 * TOPK), f32)
    return pl.pallas_call(
        target_kernel,
        out_shape=(
            jax.ShapeDtypeStruct((COLS, TOK), f32),
            jax.ShapeDtypeStruct((COLS, TOK), f32),
            jax.ShapeDtypeStruct((1, TOK), f32),
            stored,
            stored,
        ),
        in_specs=[pl.BlockSpec(memory_space=pltpu.SMEM)] + [whole()] * NY,
        out_specs=(whole(),) * 5,
        scratch_shapes=[pltpu.VMEM((TOPK, TOK), jnp.int32), pltpu.VMEM((TOPK, TOK), f32)],
        compiler_params=params(),
        cost_estimate=cost(TARGET_COST, 1_400_000),
        name="target",
    )(start, *packs)


def unpack_kernel(place, kept, passed, ids, logits, rows):
    y, c = place[2], place[3]
    for d in range(NY):
        source = ((y + NY - d) & (NY - 1)) * (NC * CAP)
        at = slice(d * CAP, (d + 1) * CAP)
        rows[pl.ds(source + c * CAP, CAP), :] = kept[at, :]
        rows[pl.ds(source + (1 - c) * CAP, CAP), :] = passed[at, :]
    ids[...] = rows[:, :TOPK].astype(jnp.int32)
    logits[...] = rows[:, TOPK:].astype(bf16)


def unpacked(place, kept, passed):
    rows = NY * NC * CAP
    return pl.pallas_call(
        unpack_kernel,
        out_shape=(
            jax.ShapeDtypeStruct((rows, TOPK), jnp.int32),
            jax.ShapeDtypeStruct((rows, TOPK), bf16),
        ),
        in_specs=[pl.BlockSpec(memory_space=pltpu.SMEM), whole(), whole()],
        out_specs=(whole(), whole()),
        scratch_shapes=[pltpu.VMEM((rows, 2 * TOPK), f32)],
        compiler_params=params(),
        name="unpack",
    )(place, kept, passed)


def logits_kernel(h0, h1, h2, h3, wo, wp, to, tp, lo, lp, stats, hid):
    step = pl.program_id(0)
    h = jnp.concatenate([h0[...], h1[...], h2[...], h3[...]], axis=0)
    hid[...] = h
    dims = (((1,), (1,)), ((), ()))
    a = lax.dot_general(wo[...], h, dims, preferred_element_type=f32)
    b = lax.dot_general(wp[...], h, dims, preferred_element_type=f32)

    @pl.when(step == 0)
    def _():
        lo[...] = a
        lp[...] = b

    @pl.when(step > 0)
    def _():
        lo[...] += a
        lp[...] += b

    @pl.when(step == pl.num_programs(0) - 1)
    def _():
        own, par = lo[...], lp[...]
        peak = jnp.maximum(
            jnp.max(own, axis=0, keepdims=True), jnp.max(par, axis=0, keepdims=True)
        )
        total = jnp.sum(jnp.exp(own - peak), axis=0, keepdims=True) + jnp.sum(
            jnp.exp(par - peak), axis=0, keepdims=True
        )
        cross = jnp.sum(own * to[...], axis=0, keepdims=True) + jnp.sum(
            par * tp[...], axis=0, keepdims=True
        )
        stats[...] = jnp.concatenate([peak, total, cross, jnp.zeros((5, TOK), f32)], axis=0)


def logits_of(blocks, wo, wp, to, tp):
    steps = 2
    k = D // steps
    fixed = lambda shape: pl.BlockSpec(shape, lambda i: (0, 0))
    return pl.pallas_call(
        logits_kernel,
        grid=(steps,),
        out_shape=(
            jax.ShapeDtypeStruct((COLS, TOK), f32),
            jax.ShapeDtypeStruct((COLS, TOK), f32),
            jax.ShapeDtypeStruct((8, TOK), f32),
            jax.ShapeDtypeStruct((TOK, D), bf16),
        ),
        in_specs=[pl.BlockSpec((ROWS, k), lambda i: (0, i))] * 4
        + [pl.BlockSpec((COLS, k), lambda i: (0, i))] * 2
        + [fixed((COLS, TOK))] * 2,
        out_specs=(
            fixed((COLS, TOK)),
            fixed((COLS, TOK)),
            fixed((8, TOK)),
            pl.BlockSpec((TOK, k), lambda i: (0, i)),
        ),
        compiler_params=params(),
        cost_estimate=cost(2 * TOK * D * COLS * 2, 14_000_000),
        name="logits",
    )(*blocks, wo, wp, to, tp)


def merge(parts):
    peak = parts[0][0:1]
    for p in parts[1:]:
        peak = jnp.maximum(peak, p[0:1])
    total = sum(p[1:2] * jnp.exp(p[0:1] - peak) for p in parts)
    cross = sum(p[2:3] for p in parts)
    return peak, total, cross


def merge_kernel(shifts, *refs):
    parts = []
    for ref, shift in zip(refs[:-1], shifts):
        part = ref[...]
        if shift:
            part = pltpu.roll(part, TOK - shift * ROWS, 1)
        parts.append(part)
    peak, total, cross = merge(parts)
    refs[-1][...] = jnp.concatenate([peak, total, cross, jnp.zeros((5, TOK), f32)], axis=0)


def merged(parts, shifts):
    return pl.pallas_call(
        functools.partial(merge_kernel, shifts),
        out_shape=jax.ShapeDtypeStruct((8, TOK), f32),
        in_specs=[whole()] * len(parts),
        out_specs=whole(),
        compiler_params=params(),
        name="merge",
    )(*parts)


def row_block(peak, total, cross):
    return jnp.concatenate([peak, total, cross, jnp.zeros((5, TOK), f32)], axis=0)


def ring_kernel(before, here, after, three, two):
    b, h, a = before[...], here[...], after[...]
    three[...] = row_block(*merge([b, h, a]))
    two[...] = row_block(*merge([h, a]))


def ring_merged(before, here, after):
    return pl.pallas_call(
        ring_kernel,
        out_shape=[jax.ShapeDtypeStruct((8, TOK), f32)] * 2,
        in_specs=[whole()] * 3,
        out_specs=[whole()] * 2,
        compiler_params=params(),
        name="ring_merge",
    )(before, here, after)


def final_kernel(tk, *refs):
    peak, total, cross = merge([ref[...] for ref in refs[:-1]])
    norm = peak + jnp.log(total)
    refs[-1][...] = jnp.concatenate(
        [norm, tk[...] + norm - cross, jnp.zeros((6, TOK), f32)], axis=0
    )


def final_norm(tk, parts):
    return pl.pallas_call(
        final_kernel,
        out_shape=jax.ShapeDtypeStruct((8, TOK), f32),
        in_specs=[whole()] * (len(parts) + 1),
        out_specs=whole(),
        compiler_params=params(),
        name="norm",
    )(tk, *parts)


def gradient_kernel(lo, lp, to, tp, norm, go, gp, g_own, g_par):
    n = norm[0:1, :]
    own = (loss_scale * (jnp.exp(lo[...] - n) - to[...])).astype(bf16)
    par = (loss_scale * (jnp.exp(lp[...] - n) - tp[...])).astype(bf16)
    go[...] = own
    gp[...] = par
    g_own[...] = own.T
    g_par[...] = par.T


def gradient_of(lo, lp, to, tp, norm):
    return pl.pallas_call(
        gradient_kernel,
        out_shape=[jax.ShapeDtypeStruct((COLS, TOK), bf16)] * 2
        + [jax.ShapeDtypeStruct((TOK, COLS), bf16)] * 2,
        in_specs=[whole()] * 5,
        out_specs=[whole()] * 4,
        compiler_params=params(),
        cost_estimate=cost(0, 4_000_000),
        name="gradient",
    )(lo, lp, to, tp, norm)


def terms_kernel(place, g_own, g_par, wo, wp, *rest):
    outs_a, outs_b = rest[0:4], rest[4:8]
    x = place[1]

    def features(ref, e):
        return jnp.concatenate(
            [
                ref[:, pl.ds(pl.multiple_of((e * NX + ((x + d) & (NX - 1))) * 128, 128), 128)]
                for d in range(NX)
            ],
            axis=1,
        )

    for e in range(ZSTEP):
        out = jnp.dot(g_own[...], features(wo, e), preferred_element_type=f32)
        out = out + jnp.dot(g_par[...], features(wp, e), preferred_element_type=f32)
        at = slice(e * 128, (e + 1) * 128)
        for d in range(NX):
            for r in range(NY):
                piece = out[r * ROWS : (r + 1) * ROWS, d * 128 : (d + 1) * 128]
                outs_a[d][r, :, at] = piece[:HALF].astype(outs_a[d].dtype)
                outs_b[r][d, :, at] = piece[HALF:].astype(outs_b[r].dtype)


def terms_of(place, g_own, g_par, wo, wp):
    wide = pl.BlockSpec((COLS, ZSTEP * NX * 128), lambda e, place: (0, e))
    piece = pl.BlockSpec((4, HALF, ZSTEP * 128), lambda e, place: (0, 0, e))
    out = [jax.ShapeDtypeStruct((4, HALF, NZ * 128), t) for t in (f32, bf16, bf16, bf16)]
    return pl.pallas_call(
        terms_kernel,
        grid_spec=pltpu.PrefetchScalarGridSpec(
            num_scalar_prefetch=1,
            grid=(NZ // ZSTEP,),
            in_specs=[pl.BlockSpec((TOK, COLS), lambda e, place: (0, 0))] * 2 + [wide, wide],
            out_specs=[piece] * 8,
        ),
        out_shape=out + out,
        compiler_params=params(),
        cost_estimate=cost(2 * TOK * D * COLS * 2, 16_000_000),
        name="terms",
    )(place, g_own, g_par, wo, wp)


def sum_first_kernel(*refs):
    for half in range(2):
        ins, outs = refs[4 * half : 4 * half + 4], refs[8 + 4 * half : 12 + 4 * half]
        for r in range(4):
            total = ins[0][r]
            for ref in ins[1:]:
                total = total + ref[r].astype(f32)
            outs[r][...] = total


def sum_first(a, b):
    out = jax.ShapeDtypeStruct((HALF, NZ * 128), f32)
    res = pl.pallas_call(
        sum_first_kernel,
        out_shape=[out] * 8,
        in_specs=[whole()] * 8,
        out_specs=[whole()] * 8,
        compiler_params=params(),
        name="sum_first",
    )(*a, *b)
    return res[:4], res[4:]


def sum_second_kernel(place, *refs):
    ins_a, ins_b, outs = refs[0:4], refs[4:8], refs[8:]
    spots = ((0, 0), (1, 0), (3, 0), (3, 1), (3, 2), (4, 0), (4, 1), (2, 0))
    for e in range(NZ):
        at = pl.ds(pl.multiple_of(((place[0] + e) & (NZ - 1)) * 128, 128), 128)
        k, i = spots[e]
        outs[k][i, :HALF] = ins_a[0][:, at] + ins_a[1][:, at] + ins_a[2][:, at] + ins_a[3][:, at]
        outs[k][i, HALF:] = ins_b[0][:, at] + ins_b[1][:, at] + ins_b[2][:, at] + ins_b[3][:, at]


def sum_second(place, a, b):
    return pl.pallas_call(
        sum_second_kernel,
        out_shape=[jax.ShapeDtypeStruct((n, ROWS, 128), f32) for n in (1, 1, 1, 3, 2)],
        in_specs=[pl.BlockSpec(memory_space=pltpu.SMEM)] + [whole()] * 8,
        out_specs=[whole()] * 5,
        compiler_params=params(),
        name="sum_second",
    )(place, *a, *b)


def sum_third_kernel(own, ahead, behind, three, two, out_own, out_ahead, out_behind):
    out_own[...] = own[...] + three[1:2] + two[0:1]
    out_ahead[...] = ahead[...] + three[2:3] + two[1:2]
    out_behind[...] = behind[...] + three[0:1]


def sum_third(*values):
    return pl.pallas_call(
        sum_third_kernel,
        out_shape=[jax.ShapeDtypeStruct((1, ROWS, 128), f32)] * 3,
        in_specs=[whole()] * 5,
        out_specs=[whole()] * 3,
        compiler_params=params(),
        name="sum_third",
    )(*values)


def head_kernel(g0, g1, h0, h1, out):
    total = jnp.dot(g0[...], h0[...], preferred_element_type=f32)
    total = total + jnp.dot(g1[...], h1[...], preferred_element_type=f32)
    out[...] = total.astype(bf16)


def head_grad(g0, g1, h0, h1):
    width = 1024
    return pl.pallas_call(
        head_kernel,
        grid=(D // width,),
        out_shape=jax.ShapeDtypeStruct((COLS, D), bf16),
        in_specs=[pl.BlockSpec((COLS, TOK), lambda i: (0, 0))] * 2
        + [pl.BlockSpec((TOK, width), lambda i: (0, i))] * 2,
        out_specs=pl.BlockSpec((COLS, width), lambda i: (0, i)),
        compiler_params=params(),
        cost_estimate=cost(4 * TOK * D * COLS, 10_000_000),
        name="head_grad",
    )(g0, g1, h0, h1)


def tied(*values):
    return lax.optimization_barrier(values)


def body(hidden, head_weight, teacher_ids, teacher_logits, labels, store_ids, store_logits, owner):
    y, c, z, x = (lax.axis_index(name).astype(jnp.int32) for name in AXES)
    place = jnp.stack([z, x, y, c])
    start = jnp.stack([index_of(y, c, z, x) * COLS, index_of(y, c + 1, z, x) * COLS])
    w_own = jnp.transpose(head_weight)

    packs = packs_of(
        place, owner[:, 0], teacher_ids, teacher_logits, labels[None, :], store_ids, store_logits
    )
    opposite = send(hidden, dy=2)
    packs = [send(p, dy=d) if d else p for d, p in enumerate(packs)]
    *packs, nearby = tied(*packs, hidden)
    blocks = [hidden, send(nearby, dy=1), opposite, send(nearby, dy=3)]
    w_par = send(w_own, dc=1)
    to, tp, tk, kept, passed = target_of(start, packs)
    next_ids, next_logits = unpacked(place, kept, send(passed, dc=1))
    tp, next_ids, next_logits = tied(tp, next_ids, next_logits)
    lo, lp, stats, hid = logits_of(blocks, w_own, w_par, to, tp)

    parts = [stats] + [send(stats, dx=d) for d in range(1, NX)]
    stats = merged(parts, (0,) * NX)
    parts = [stats] + [send(stats, dy=-d) for d in range(1, NY)]
    stats = merged(parts, tuple(range(NY)))
    hid_par = send(hid, dc=1)
    three, two = ring_merged(send(stats, dz=1), stats, send(stats, dz=-1))
    norm = final_norm(tk, [three, send(three, dz=-3), send(two, dz=3)])
    norm, hid_par = tied(norm, hid_par)
    token_loss = norm[1, :ROWS]

    go, gp, g_own, g_par = gradient_of(lo, lp, to, tp, norm)
    g_other = send(gp, dc=1)
    terms = list(terms_of(place, g_own, g_par, w_own, w_par))
    terms[1], g_other = tied(terms[1], g_other)
    a, b = terms[0:4], terms[4:8]
    a = [a[0]] + [send(a[d], dx=d) for d in range(1, NX)]
    b = [b[0]] + [send(b[d], dy=-d) for d in range(1, NY)]
    grad_head = head_grad(go, g_other, hid, hid_par)
    *received, grad_head = tied(*a[1:], *b[1:], grad_head)
    a, b = sum_first([a[0]] + received[0:3], [b[0]] + received[3:6])
    grad_head = jnp.transpose(grad_head)
    a = [a[0]] + [send(a[d], dy=-d) for d in range(1, NY)]
    b = [b[0]] + [send(b[d], dx=d) for d in range(1, NX)]
    own, ahead, behind, three, two = sum_second(place, a, b)
    own, ahead, behind = sum_third(own, ahead, behind, send(three, dz=3), send(two, dz=-3))
    grad_hidden = own + send(ahead, dz=1) + send(behind, dz=-1)
    grad_hidden = grad_hidden.reshape(ROWS, 128).astype(bf16)
    return (grad_head, grad_hidden, token_loss, next_ids, next_logits)


def solution(mesh):
    fine = jax.sharding.Mesh(mesh.devices.reshape(NY, NC, NZ, NX), AXES)
    dp, vocab, both = ("y", "c"), ("z", "x"), AXES
    return jax.shard_map(
        body,
        mesh=fine,
        in_specs=(
            P(dp, None),
            P(None, both),
            P(dp, None),
            P(dp, None),
            P(dp),
            P(both, None),
            P(both, None),
            P(both, None),
        ),
        out_specs=(
            P(None, both),
            P(dp, vocab),
            P(dp),
            P(both, None),
            P(both, None),
        ),
        check_vma=False,
    )
```

```python
import functools

import jax
import jax.numpy as jnp
from jax import lax
from jax.experimental import pallas as pl
from jax.experimental.pallas import tpu as pltpu
from jax.sharding import PartitionSpec as P

mixing = 0.5
loss_scale = 64.0
f32 = jnp.float32
bf16 = jnp.bfloat16
NY, NC, NZ, NX = 4, 2, 8, 4
AXES = ("y", "c", "z", "x")
ROWS = 64
TOK = NY * ROWS
D = 4096
COLS = 592
TOPK = 64
CAP = 4
HALF = ROWS // 2
VMEM = 48 * 1024 * 1024
ZSTEP = 4
TARGET_COST = 1_000_000


def index_of(y, c, z, x):
    return (((y % NY) * NC + c % NC) * NZ + z % NZ) * NX + x % NX


def send(value, dy=0, dc=0, dz=0, dx=0):
    pairs = [
        (index_of(y, c, z, x), index_of(y + dy, c + dc, z + dz, x + dx))
        for y in range(NY)
        for c in range(NC)
        for z in range(NZ)
        for x in range(NX)
    ]
    return lax.ppermute(value, AXES, pairs)


def swap_x(value):
    pairs = [
        (index_of(y, c, z, x), index_of(y, c, z, x ^ 1))
        for y in range(NY)
        for c in range(NC)
        for z in range(NZ)
        for x in range(NX)
    ]
    return lax.ppermute(value, AXES, pairs)


def params(size=VMEM):
    return pltpu.CompilerParams(vmem_limit_bytes=size)


def whole():
    return pl.BlockSpec(memory_space=pltpu.VMEM)


def cost(flops, size):
    return pl.CostEstimate(flops=flops, bytes_accessed=size, transcendentals=0)


def pack_kernel(place, owner, ids, scores, label, store_ids, store_logits, *outs):
    y, c = place[2], place[3]
    entries = jnp.concatenate([ids[...].astype(f32), scores[...].astype(f32)], axis=1).T
    teacher = jnp.concatenate([entries[:TOPK], entries[TOPK:]], axis=1)
    label_rows = jnp.concatenate([label[...].astype(f32), jnp.zeros((1, ROWS), f32)], axis=1)
    label_rows = jnp.concatenate([label_rows, jnp.zeros((7, 2 * ROWS), f32)], axis=0)
    lane = lax.broadcasted_iota(jnp.int32, (NC * CAP, 2 * TOPK), 1)
    empty = jnp.where(lane < TOPK, -1.0, 0.0)
    for out in outs:
        out[0:TOPK, :] = teacher
        out[TOPK : TOPK + 8, :] = label_rows
        out[TOPK + 8 : TOPK + 16, :] = empty
    rows = store_ids.shape[0]
    values = jnp.concatenate(
        [store_ids[...].astype(f32), store_logits[...].astype(f32)], axis=1
    )
    for j in range(rows):
        named = owner[j]
        slot = jnp.int32(0)
        for i in range(j):
            slot = slot + (owner[i] == named).astype(jnp.int32)
        ahead = ((named >> 1) + NY - y) & (NY - 1)
        row = TOPK + 8 + ((named + c) & 1) * CAP + slot
        for d in range(NY):

            @pl.when(ahead == d)
            def _(out=outs[d], row=row, j=j):
                out[pl.ds(row, 1), :] = values[j : j + 1, :]


def packs_of(place, owner, ids, scores, label, store_ids, store_logits):
    smem = pl.BlockSpec(memory_space=pltpu.SMEM)
    return pl.pallas_call(
        pack_kernel,
        out_shape=[jax.ShapeDtypeStruct((TOPK + 16, 2 * TOPK), f32)] * NY,
        in_specs=[smem, smem] + [whole()] * 5,
        out_specs=[whole()] * NY,
        compiler_params=params(60 * 1024 * 1024),
        name="pack",
    )(place, owner, ids, scores, label, store_ids, store_logits)


def target_kernel(start_ref, p0, p1, p2, p3, own_ref, par_ref, tk_ref, kept_ref, pass_ref, ids_ref, prob_ref):
    packs = (p0, p1, p2, p3)
    ids_ref[...] = jnp.concatenate([p[0:TOPK, :ROWS] for p in packs], axis=1).astype(jnp.int32)
    scores = jnp.concatenate([p[0:TOPK, ROWS:] for p in packs], axis=1)
    label = jnp.concatenate([p[TOPK : TOPK + 1, :ROWS] for p in packs], axis=1).astype(jnp.int32)
    for d, p in enumerate(packs):
        kept_ref[d * CAP : (d + 1) * CAP, :] = p[TOPK + 8 : TOPK + 8 + CAP, :]
    other = jnp.concatenate([p[TOPK + 8 + CAP : TOPK + 16, :] for p in packs], axis=0)
    named = other[:, :TOPK].astype(jnp.int32)
    digits = [(named >> 16), (named >> 8) & 255, named & 255]
    pass_ref[...] = jnp.concatenate(
        [v.astype(f32) for v in digits] + [other[:, TOPK:]], axis=1
    ).astype(bf16)
    shifted = scores - jnp.max(scores, axis=0, keepdims=True)
    logp = shifted - jnp.log(jnp.sum(jnp.exp(shifted), axis=0, keepdims=True))
    prob = jnp.exp(logp)
    tk_ref[...] = mixing * jnp.sum(prob * logp, axis=0, keepdims=True)
    prob_ref[...] = mixing * prob
    step = 16

    def rows(i, carry):
        first = pl.multiple_of(i * step, step)
        iota = lax.broadcasted_iota(jnp.int32, (step, TOK), 0) + first
        cols_own = iota + start_ref[0]
        cols_par = iota + start_ref[1]
        own = jnp.where(cols_own == label, 1.0 - mixing, 0.0)
        par = jnp.where(cols_par == label, 1.0 - mixing, 0.0)
        for k in range(TOPK):
            ids = ids_ref[pl.ds(k, 1), :]
            p = prob_ref[pl.ds(k, 1), :]
            own = own + jnp.where(cols_own == ids, p, 0.0)
            par = par + jnp.where(cols_par == ids, p, 0.0)
        own_ref[pl.ds(first, step), :] = own
        par_ref[pl.ds(first, step), :] = par
        return carry

    lax.fori_loop(0, COLS // step, rows, 0)


def target_of(start, packs):
    return pl.pallas_call(
        target_kernel,
        out_shape=(
            jax.ShapeDtypeStruct((COLS, TOK), f32),
            jax.ShapeDtypeStruct((COLS, TOK), f32),
            jax.ShapeDtypeStruct((1, TOK), f32),
            jax.ShapeDtypeStruct((NY * CAP, 2 * TOPK), f32),
            jax.ShapeDtypeStruct((NY * CAP, 4 * TOPK), bf16),
        ),
        in_specs=[pl.BlockSpec(memory_space=pltpu.SMEM)] + [whole()] * NY,
        out_specs=(whole(),) * 5,
        scratch_shapes=[pltpu.VMEM((TOPK, TOK), jnp.int32), pltpu.VMEM((TOPK, TOK), f32)],
        compiler_params=params(),
        cost_estimate=cost(TARGET_COST, 1_400_000),
        name="target",
    )(start, *packs)


def unpack_kernel(place, kept, digits, ids, logits, rows):
    y, c = place[2], place[3]
    high, middle, low, scores = (
        digits[:, k * TOPK : (k + 1) * TOPK].astype(f32) for k in range(4)
    )
    passed = jnp.concatenate([high * 65536.0 + (middle * 256.0 + low), scores], axis=1)
    for d in range(NY):
        source = ((y + NY - d) & (NY - 1)) * (NC * CAP)
        at = slice(d * CAP, (d + 1) * CAP)
        rows[pl.ds(source + c * CAP, CAP), :] = kept[at, :]
        rows[pl.ds(source + (1 - c) * CAP, CAP), :] = passed[at]
    ids[...] = rows[:, :TOPK].astype(jnp.int32)
    logits[...] = rows[:, TOPK:].astype(bf16)


def unpacked(place, kept, hid_par):
    rows = NY * NC * CAP
    return pl.pallas_call(
        unpack_kernel,
        out_shape=(
            jax.ShapeDtypeStruct((rows, TOPK), jnp.int32),
            jax.ShapeDtypeStruct((rows, TOPK), bf16),
        ),
        grid=(1,),
        in_specs=[
            pl.BlockSpec(memory_space=pltpu.SMEM),
            pl.BlockSpec((NY * CAP, 2 * TOPK), lambda i: (0, 0)),
            pl.BlockSpec((NY * CAP, 4 * TOPK), lambda i: (TOK // (NY * CAP), 0)),
        ],
        out_specs=(
            pl.BlockSpec((rows, TOPK), lambda i: (0, 0)),
            pl.BlockSpec((rows, TOPK), lambda i: (0, 0)),
        ),
        scratch_shapes=[pltpu.VMEM((rows, 2 * TOPK), f32)],
        compiler_params=params(),
        name="unpack",
    )(place, kept, hid_par)


def logits_kernel(place, h0, h1, direct, swapped, h3, passed, wo, wp, to, tp, lo, lp, stats, hid):
    step = pl.program_id(0)
    odd = place[1] & 1
    hid[0:ROWS, :] = h0[...]
    hid[ROWS : 2 * ROWS, :] = h1[...]
    hid[pl.ds(pl.multiple_of(2 * ROWS + odd * HALF, HALF), HALF), :] = direct[...]
    hid[pl.ds(pl.multiple_of(2 * ROWS + (1 - odd) * HALF, HALF), HALF), :] = swapped[...]
    hid[3 * ROWS : TOK, :] = h3[...]
    hid[TOK:, :] = jnp.zeros((NY * CAP, hid.shape[1]), bf16)
    hid[TOK:, : 4 * TOPK] = passed[...]
    h = hid[0:TOK, :]
    dims = (((1,), (1,)), ((), ()))
    a = lax.dot_general(wo[...], h, dims, preferred_element_type=f32)
    b = lax.dot_general(wp[...], h, dims, preferred_element_type=f32)

    @pl.when(step == 0)
    def _():
        lo[...] = a
        lp[...] = b

    @pl.when(step > 0)
    def _():
        lo[...] += a
        lp[...] += b

    @pl.when(step == pl.num_programs(0) - 1)
    def _():
        own, par = lo[...], lp[...]
        peak = jnp.maximum(
            jnp.max(own, axis=0, keepdims=True), jnp.max(par, axis=0, keepdims=True)
        )
        total = jnp.sum(jnp.exp(own - peak), axis=0, keepdims=True) + jnp.sum(
            jnp.exp(par - peak), axis=0, keepdims=True
        )
        cross = jnp.sum(own * to[...], axis=0, keepdims=True) + jnp.sum(
            par * tp[...], axis=0, keepdims=True
        )
        stats[...] = jnp.concatenate([peak, total, cross, jnp.zeros((5, TOK), f32)], axis=0)


def logits_of(place, blocks, passed, wo, wp, to, tp):
    steps = 2
    k = D // steps
    fixed = lambda shape: pl.BlockSpec(shape, lambda i: (0, 0))
    return pl.pallas_call(
        logits_kernel,
        grid=(steps,),
        out_shape=(
            jax.ShapeDtypeStruct((COLS, TOK), f32),
            jax.ShapeDtypeStruct((COLS, TOK), f32),
            jax.ShapeDtypeStruct((8, TOK), f32),
            jax.ShapeDtypeStruct((TOK + NY * CAP, D), bf16),
        ),
        in_specs=[pl.BlockSpec(memory_space=pltpu.SMEM)]
        + [pl.BlockSpec((b.shape[0], k), lambda i: (0, i)) for b in blocks]
        + [fixed((NY * CAP, 4 * TOPK))]
        + [pl.BlockSpec((COLS, k), lambda i: (0, i))] * 2
        + [fixed((COLS, TOK))] * 2,
        out_specs=(
            fixed((COLS, TOK)),
            fixed((COLS, TOK)),
            fixed((8, TOK)),
            pl.BlockSpec((TOK + NY * CAP, k), lambda i: (0, i)),
        ),
        compiler_params=params(),
        cost_estimate=cost(2 * TOK * D * COLS * 2, 14_000_000),
        name="logits",
    )(place, *blocks, passed, wo, wp, to, tp)


def merge(parts):
    peak = parts[0][0:1]
    for p in parts[1:]:
        peak = jnp.maximum(peak, p[0:1])
    total = sum(p[1:2] * jnp.exp(p[0:1] - peak) for p in parts)
    cross = sum(p[2:3] for p in parts)
    return peak, total, cross


def merge_kernel(shifts, *refs):
    parts = []
    for ref, shift in zip(refs[:-1], shifts):
        part = ref[...]
        if shift:
            part = pltpu.roll(part, TOK - shift * ROWS, 1)
        parts.append(part)
    peak, total, cross = merge(parts)
    refs[-1][...] = jnp.concatenate([peak, total, cross, jnp.zeros((5, TOK), f32)], axis=0)


def merged(parts, shifts):
    return pl.pallas_call(
        functools.partial(merge_kernel, shifts),
        out_shape=jax.ShapeDtypeStruct((8, TOK), f32),
        in_specs=[whole()] * len(parts),
        out_specs=whole(),
        compiler_params=params(),
        name="merge",
    )(*parts)


def row_block(peak, total, cross):
    return jnp.concatenate([peak, total, cross, jnp.zeros((5, TOK), f32)], axis=0)


def ring_kernel(before, here, after, three, two):
    b, h, a = before[...], here[...], after[...]
    three[...] = row_block(*merge([b, h, a]))
    two[...] = row_block(*merge([h, a]))


def ring_merged(before, here, after):
    return pl.pallas_call(
        ring_kernel,
        out_shape=[jax.ShapeDtypeStruct((8, TOK), f32)] * 2,
        in_specs=[whole()] * 3,
        out_specs=[whole()] * 2,
        compiler_params=params(),
        name="ring_merge",
    )(before, here, after)


def final_kernel(tk, *refs):
    peak, total, cross = merge([ref[...] for ref in refs[:-1]])
    norm = peak + jnp.log(total)
    refs[-1][...] = jnp.concatenate(
        [norm, tk[...] + norm - cross, jnp.zeros((6, TOK), f32)], axis=0
    )


def final_norm(tk, parts):
    return pl.pallas_call(
        final_kernel,
        out_shape=jax.ShapeDtypeStruct((8, TOK), f32),
        in_specs=[whole()] * (len(parts) + 1),
        out_specs=whole(),
        compiler_params=params(),
        name="norm",
    )(tk, *parts)


def gradient_kernel(lo, lp, to, tp, norm, go, gp, g_own, g_par):
    n = norm[0:1, :]
    own = (loss_scale * (jnp.exp(lo[...] - n) - to[...])).astype(bf16)
    par = (loss_scale * (jnp.exp(lp[...] - n) - tp[...])).astype(bf16)
    go[...] = own
    gp[...] = par
    g_own[...] = own.T
    g_par[...] = par.T


def gradient_of(lo, lp, to, tp, norm):
    return pl.pallas_call(
        gradient_kernel,
        out_shape=[jax.ShapeDtypeStruct((COLS, TOK), bf16)] * 2
        + [jax.ShapeDtypeStruct((TOK, COLS), bf16)] * 2,
        in_specs=[whole()] * 5,
        out_specs=[whole()] * 4,
        compiler_params=params(),
        cost_estimate=cost(0, 4_000_000),
        name="gradient",
    )(lo, lp, to, tp, norm)


def terms_kernel(place, g_own, g_par, wo, wp, *rest):
    outs_a, outs_b = rest[0:4], rest[4:8]
    x = place[1]

    def features(ref, e):
        return jnp.concatenate(
            [
                ref[:, pl.ds(pl.multiple_of((e * NX + ((x + d) & (NX - 1))) * 128, 128), 128)]
                for d in range(NX)
            ],
            axis=1,
        )

    for e in range(ZSTEP):
        out = jnp.dot(g_own[...], features(wo, e), preferred_element_type=f32)
        out = out + jnp.dot(g_par[...], features(wp, e), preferred_element_type=f32)
        at = slice(e * 128, (e + 1) * 128)
        for d in range(NX):
            for r in range(NY):
                piece = out[r * ROWS : (r + 1) * ROWS, d * 128 : (d + 1) * 128]
                outs_a[d][r, :, at] = piece[:HALF].astype(outs_a[d].dtype)
                outs_b[r][d, :, at] = piece[HALF:].astype(outs_b[r].dtype)


def terms_of(place, g_own, g_par, wo, wp):
    wide = pl.BlockSpec((COLS, ZSTEP * NX * 128), lambda e, place: (0, e))
    piece = pl.BlockSpec((4, HALF, ZSTEP * 128), lambda e, place: (0, 0, e))
    out = [jax.ShapeDtypeStruct((4, HALF, NZ * 128), t) for t in (f32, bf16, bf16, bf16)]
    return pl.pallas_call(
        terms_kernel,
        grid_spec=pltpu.PrefetchScalarGridSpec(
            num_scalar_prefetch=1,
            grid=(NZ // ZSTEP,),
            in_specs=[pl.BlockSpec((TOK, COLS), lambda e, place: (0, 0))] * 2 + [wide, wide],
            out_specs=[piece] * 8,
        ),
        out_shape=out + out,
        compiler_params=params(),
        cost_estimate=cost(2 * TOK * D * COLS * 2, 16_000_000),
        name="terms",
    )(place, g_own, g_par, wo, wp)


def sum_first_kernel(*refs):
    for half in range(2):
        ins, outs = refs[4 * half : 4 * half + 4], refs[8 + 4 * half : 12 + 4 * half]
        for r in range(4):
            total = ins[0][r]
            for ref in ins[1:]:
                total = total + ref[r].astype(f32)
            outs[r][...] = total


def sum_first(a, b):
    out = jax.ShapeDtypeStruct((HALF, NZ * 128), f32)
    res = pl.pallas_call(
        sum_first_kernel,
        out_shape=[out] * 8,
        in_specs=[whole()] * 8,
        out_specs=[whole()] * 8,
        compiler_params=params(),
        name="sum_first",
    )(*a, *b)
    return res[:4], res[4:]


def sum_second_kernel(place, *refs):
    ins_a, ins_b, outs = refs[0:4], refs[4:8], refs[8:]
    spots = ((0, 0), (1, 0), (3, 0), (3, 1), (3, 2), (4, 0), (4, 1), (2, 0))
    for e in range(NZ):
        at = pl.ds(pl.multiple_of(((place[0] + e) & (NZ - 1)) * 128, 128), 128)
        k, i = spots[e]
        outs[k][i, :HALF] = ins_a[0][:, at] + ins_a[1][:, at] + ins_a[2][:, at] + ins_a[3][:, at]
        outs[k][i, HALF:] = ins_b[0][:, at] + ins_b[1][:, at] + ins_b[2][:, at] + ins_b[3][:, at]


def sum_second(place, a, b):
    return pl.pallas_call(
        sum_second_kernel,
        out_shape=[jax.ShapeDtypeStruct((n, ROWS, 128), f32) for n in (1, 1, 1, 3, 2)],
        in_specs=[pl.BlockSpec(memory_space=pltpu.SMEM)] + [whole()] * 8,
        out_specs=[whole()] * 5,
        compiler_params=params(),
        name="sum_second",
    )(place, *a, *b)


def sum_third_kernel(own, ahead, behind, three, two, out_own, out_ahead, out_behind):
    out_own[...] = own[...] + three[1:2] + two[0:1]
    out_ahead[...] = ahead[...] + three[2:3] + two[1:2]
    out_behind[...] = behind[...] + three[0:1]


def sum_third(*values):
    return pl.pallas_call(
        sum_third_kernel,
        out_shape=[jax.ShapeDtypeStruct((1, ROWS, 128), f32)] * 3,
        in_specs=[whole()] * 5,
        out_specs=[whole()] * 3,
        compiler_params=params(),
        name="sum_third",
    )(*values)


def head_kernel(g0, g1, h0, h1, out):
    total = jnp.dot(g0[...], h0[...], preferred_element_type=f32)
    total = total + jnp.dot(g1[...], h1[...], preferred_element_type=f32)
    out[...] = total.astype(bf16)


def head_grad(g0, g1, h0, h1):
    width = 1024
    return pl.pallas_call(
        head_kernel,
        grid=(D // width,),
        out_shape=jax.ShapeDtypeStruct((COLS, D), bf16),
        in_specs=[pl.BlockSpec((COLS, TOK), lambda i: (0, 0))] * 2
        + [pl.BlockSpec((TOK, width), lambda i: (0, i))] * 2,
        out_specs=pl.BlockSpec((COLS, width), lambda i: (0, i)),
        compiler_params=params(),
        cost_estimate=cost(4 * TOK * D * COLS, 10_000_000),
        name="head_grad",
    )(g0, g1, h0, h1)


def tied(*values):
    return lax.optimization_barrier(values)


def body(hidden, head_weight, teacher_ids, teacher_logits, labels, store_ids, store_logits, owner):
    y, c, z, x = (lax.axis_index(name).astype(jnp.int32) for name in AXES)
    place = jnp.stack([z, x, y, c])
    start = jnp.stack([index_of(y, c, z, x) * COLS, index_of(y, c + 1, z, x) * COLS])
    w_own = jnp.transpose(head_weight)

    packs = packs_of(
        place, owner[:, 0], teacher_ids, teacher_logits, labels[None, :], store_ids, store_logits
    )
    half = lax.dynamic_slice_in_dim(hidden, (x % 2) * HALF, HALF, 0)
    direct = send(half, dy=2)
    packs = [send(p, dy=d) if d else p for d, p in enumerate(packs)]
    *packs, direct, nearby = tied(*packs, direct, hidden)
    swapped = swap_x(direct)
    blocks = [hidden, send(nearby, dy=1), direct, swapped, send(nearby, dy=3)]
    w_par = send(w_own, dc=1)
    to, tp, tk, kept, passed = target_of(start, packs)
    lo, lp, stats, hid = logits_of(place, blocks, passed, w_own, w_par, to, tp)

    parts = [stats] + [send(stats, dx=d) for d in range(1, NX)]
    stats = merged(parts, (0,) * NX)
    parts = [stats] + [send(stats, dy=-d) for d in range(1, NY)]
    stats = merged(parts, tuple(range(NY)))
    hid_par = send(hid, dc=1)
    three, two = ring_merged(send(stats, dz=1), stats, send(stats, dz=-1))
    norm = final_norm(tk, [three, send(three, dz=-3), send(two, dz=3)])
    norm, hid_par = tied(norm, hid_par)
    next_ids, next_logits = unpacked(place, kept, hid_par)
    token_loss = norm[1, :ROWS]

    go, gp, g_own, g_par = gradient_of(lo, lp, to, tp, norm)
    g_other = send(gp, dc=1)
    terms = list(terms_of(place, g_own, g_par, w_own, w_par))
    terms[1], g_other = tied(terms[1], g_other)
    a, b = terms[0:4], terms[4:8]
    a = [a[0]] + [send(a[d], dx=d) for d in range(1, NX)]
    b = [b[0]] + [send(b[d], dy=-d) for d in range(1, NY)]
    grad_head = head_grad(go, g_other, hid, hid_par)
    *received, grad_head, next_ids, next_logits = tied(
        *a[1:], *b[1:], grad_head, next_ids, next_logits
    )
    a, b = sum_first([a[0]] + received[0:3], [b[0]] + received[3:6])
    grad_head = jnp.transpose(grad_head)
    a = [a[0]] + [send(a[d], dy=-d) for d in range(1, NY)]
    b = [b[0]] + [send(b[d], dx=d) for d in range(1, NX)]
    own, ahead, behind, three, two = sum_second(place, a, b)
    own, ahead, behind = sum_third(own, ahead, behind, send(three, dz=3), send(two, dz=-3))
    grad_hidden = own + send(ahead, dz=1) + send(behind, dz=-1)
    grad_hidden = grad_hidden.reshape(ROWS, 128).astype(bf16)
    return (grad_head, grad_hidden, token_loss, next_ids, next_logits)


def solution(mesh):
    fine = jax.sharding.Mesh(mesh.devices.reshape(NY, NC, NZ, NX), AXES)
    dp, vocab, both = ("y", "c"), ("z", "x"), AXES
    return jax.shard_map(
        body,
        mesh=fine,
        in_specs=(
            P(dp, None),
            P(None, both),
            P(dp, None),
            P(dp, None),
            P(dp),
            P(both, None),
            P(both, None),
            P(both, None),
        ),
        out_specs=(
            P(None, both),
            P(dp, vocab),
            P(dp),
            P(both, None),
            P(both, None),
        ),
        check_vma=False,
    )
```

```python
import functools

import jax
import jax.numpy as jnp
from jax import lax
from jax.experimental import pallas as pl
from jax.experimental.pallas import tpu as pltpu
from jax.sharding import PartitionSpec as P

mixing = 0.5
loss_scale = 64.0
f32 = jnp.float32
bf16 = jnp.bfloat16
NY, NC, NZ, NX = 4, 2, 8, 4
AXES = ("y", "c", "z", "x")
ROWS = 64
TOK = NY * ROWS
D = 4096
COLS = 592
TOPK = 64
CAP = 4
HALF = ROWS // 2
VMEM = 48 * 1024 * 1024
ZSTEP = 4
TARGET_COST = 1_000_000


def index_of(y, c, z, x):
    return (((y % NY) * NC + c % NC) * NZ + z % NZ) * NX + x % NX


def send(value, dy=0, dc=0, dz=0, dx=0):
    pairs = [
        (index_of(y, c, z, x), index_of(y + dy, c + dc, z + dz, x + dx))
        for y in range(NY)
        for c in range(NC)
        for z in range(NZ)
        for x in range(NX)
    ]
    return lax.ppermute(value, AXES, pairs)


def swap_x(value):
    pairs = [
        (index_of(y, c, z, x), index_of(y, c, z, x ^ 1))
        for y in range(NY)
        for c in range(NC)
        for z in range(NZ)
        for x in range(NX)
    ]
    return lax.ppermute(value, AXES, pairs)


def params(size=VMEM):
    return pltpu.CompilerParams(vmem_limit_bytes=size)


def whole():
    return pl.BlockSpec(memory_space=pltpu.VMEM)


def cost(flops, size):
    return pl.CostEstimate(flops=flops, bytes_accessed=size, transcendentals=0)


def pack_kernel(place, owner, ids, scores, label, store_ids, store_logits, *outs):
    y, c = place[0], place[1]
    entries = jnp.concatenate([ids[...].astype(f32), scores[...].astype(f32)], axis=1).T
    teacher = jnp.concatenate([entries[:TOPK], entries[TOPK:]], axis=1)
    label_rows = jnp.concatenate([label[...].astype(f32), jnp.zeros((1, ROWS), f32)], axis=1)
    label_rows = jnp.concatenate([label_rows, jnp.zeros((7, 2 * ROWS), f32)], axis=0)
    lane = lax.broadcasted_iota(jnp.int32, (NC * CAP, 2 * TOPK), 1)
    empty = jnp.where(lane < TOPK, -1.0, 0.0)
    for out in outs:
        out[0:TOPK, :] = teacher
        out[TOPK : TOPK + 8, :] = label_rows
        out[TOPK + 8 : TOPK + 16, :] = empty
    rows = store_ids.shape[0]
    values = jnp.concatenate(
        [store_ids[...].astype(f32), store_logits[...].astype(f32)], axis=1
    )
    for j in range(rows):
        named = owner[j]
        slot = jnp.int32(0)
        for i in range(j):
            slot = slot + (owner[i] == named).astype(jnp.int32)
        ahead = ((named >> 1) + NY - y) & (NY - 1)
        row = TOPK + 8 + ((named + c) & 1) * CAP + slot
        for d in range(NY):

            @pl.when(ahead == d)
            def _(out=outs[d], row=row, j=j):
                out[pl.ds(row, 1), :] = values[j : j + 1, :]


def packs_of(place, owner, ids, scores, label, store_ids, store_logits):
    smem = pl.BlockSpec(memory_space=pltpu.SMEM)
    return pl.pallas_call(
        pack_kernel,
        out_shape=[jax.ShapeDtypeStruct((TOPK + 16, 2 * TOPK), f32)] * NY,
        in_specs=[smem, smem] + [whole()] * 5,
        out_specs=[whole()] * NY,
        compiler_params=params(60 * 1024 * 1024),
        name="pack",
    )(place, owner, ids, scores, label, store_ids, store_logits)


def target_kernel(start_ref, p0, p1, p2, p3, own_ref, par_ref, tk_ref, kept_ref, pass_ref, ids_ref, prob_ref):
    packs = (p0, p1, p2, p3)
    ids_ref[...] = jnp.concatenate([p[0:TOPK, :ROWS] for p in packs], axis=1).astype(jnp.int32)
    scores = jnp.concatenate([p[0:TOPK, ROWS:] for p in packs], axis=1)
    label = jnp.concatenate([p[TOPK : TOPK + 1, :ROWS] for p in packs], axis=1).astype(jnp.int32)
    for d, p in enumerate(packs):
        kept_ref[d * CAP : (d + 1) * CAP, :] = p[TOPK + 8 : TOPK + 8 + CAP, :]
    other = jnp.concatenate([p[TOPK + 8 + CAP : TOPK + 16, :] for p in packs], axis=0)
    named = other[:, :TOPK].astype(jnp.int32)
    digits = [(named >> 16), (named >> 8) & 255, named & 255]
    pass_ref[...] = jnp.concatenate(
        [v.astype(f32) for v in digits] + [other[:, TOPK:]], axis=1
    ).astype(bf16)
    shifted = scores - jnp.max(scores, axis=0, keepdims=True)
    logp = shifted - jnp.log(jnp.sum(jnp.exp(shifted), axis=0, keepdims=True))
    prob = jnp.exp(logp)
    tk_ref[...] = mixing * jnp.sum(prob * logp, axis=0, keepdims=True)
    prob_ref[...] = mixing * prob
    ids_all = ids_ref[...]
    summed = jnp.zeros((TOPK, TOK), f32)
    for k in range(TOPK):
        same = ids_all == ids_ref[pl.ds(k, 1), :]
        summed = summed + jnp.where(same, prob_ref[pl.ds(k, 1), :], 0.0)
    prob_ref[...] = summed
    step = 16

    def rows(i, carry):
        first = pl.multiple_of(i * step, step)
        iota = lax.broadcasted_iota(jnp.int32, (step, TOK), 0) + first
        cols_own = iota + start_ref[0]
        cols_par = iota + start_ref[1]
        own = jnp.zeros((step, TOK), f32)
        par = jnp.zeros((step, TOK), f32)
        for k in range(TOPK):
            ids = ids_ref[pl.ds(k, 1), :]
            p = prob_ref[pl.ds(k, 1), :]
            own = jnp.where(cols_own == ids, p, own)
            par = jnp.where(cols_par == ids, p, par)
        own_ref[pl.ds(first, step), :] = own + jnp.where(cols_own == label, 1.0 - mixing, 0.0)
        par_ref[pl.ds(first, step), :] = par + jnp.where(cols_par == label, 1.0 - mixing, 0.0)
        return carry

    lax.fori_loop(0, COLS // step, rows, 0)


def target_of(start, packs):
    return pl.pallas_call(
        target_kernel,
        out_shape=(
            jax.ShapeDtypeStruct((COLS, TOK), f32),
            jax.ShapeDtypeStruct((COLS, TOK), f32),
            jax.ShapeDtypeStruct((1, TOK), f32),
            jax.ShapeDtypeStruct((NY * CAP, 2 * TOPK), f32),
            jax.ShapeDtypeStruct((NY * CAP, 4 * TOPK), bf16),
        ),
        in_specs=[pl.BlockSpec(memory_space=pltpu.SMEM)] + [whole()] * NY,
        out_specs=(whole(),) * 5,
        scratch_shapes=[pltpu.VMEM((TOPK, TOK), jnp.int32), pltpu.VMEM((TOPK, TOK), f32)],
        compiler_params=params(),
        cost_estimate=cost(TARGET_COST, 1_400_000),
        name="target",
    )(start, *packs)


def unpack_kernel(place, kept, digits, ids, logits, rows):
    c, y = place[0], place[1]
    high, middle, low, scores = (
        digits[:, k * TOPK : (k + 1) * TOPK].astype(f32) for k in range(4)
    )
    passed = jnp.concatenate([high * 65536.0 + (middle * 256.0 + low), scores], axis=1)
    for d in range(NY):
        source = ((y + NY - d) & (NY - 1)) * (NC * CAP)
        at = slice(d * CAP, (d + 1) * CAP)
        rows[pl.ds(source + c * CAP, CAP), :] = kept[at, :]
        rows[pl.ds(source + (1 - c) * CAP, CAP), :] = passed[at]
    ids[...] = rows[:, :TOPK].astype(jnp.int32)
    logits[...] = rows[:, TOPK:].astype(bf16)


def unpacked(place, kept, hid_par):
    rows = NY * NC * CAP
    return pl.pallas_call(
        unpack_kernel,
        out_shape=(
            jax.ShapeDtypeStruct((rows, TOPK), jnp.int32),
            jax.ShapeDtypeStruct((rows, TOPK), bf16),
        ),
        grid=(1,),
        in_specs=[
            pl.BlockSpec(memory_space=pltpu.SMEM),
            pl.BlockSpec((NY * CAP, 2 * TOPK), lambda i: (0, 0)),
            pl.BlockSpec((NY * CAP, 4 * TOPK), lambda i: (TOK // (NY * CAP), 0)),
        ],
        out_specs=(
            pl.BlockSpec((rows, TOPK), lambda i: (0, 0)),
            pl.BlockSpec((rows, TOPK), lambda i: (0, 0)),
        ),
        scratch_shapes=[pltpu.VMEM((rows, 2 * TOPK), f32)],
        compiler_params=params(),
        name="unpack",
    )(place, kept, hid_par)


def logits_kernel(place, h0, h1, direct, swapped, h3, passed, wo, wp, to, tp, lo, lp, stats, hid):
    step = pl.program_id(0)
    odd = place[0]
    hid[0:ROWS, :] = h0[...]
    hid[ROWS : 2 * ROWS, :] = h1[...]
    hid[pl.ds(pl.multiple_of(2 * ROWS + odd * HALF, HALF), HALF), :] = direct[...]
    hid[pl.ds(pl.multiple_of(2 * ROWS + (1 - odd) * HALF, HALF), HALF), :] = swapped[...]
    hid[3 * ROWS : TOK, :] = h3[...]
    hid[TOK:, :] = jnp.zeros((NY * CAP, hid.shape[1]), bf16)
    hid[TOK:, : 4 * TOPK] = passed[...]
    h = hid[0:TOK, :]
    dims = (((1,), (1,)), ((), ()))
    a = lax.dot_general(wo[...], h, dims, preferred_element_type=f32)
    b = lax.dot_general(wp[...], h, dims, preferred_element_type=f32)

    @pl.when(step == 0)
    def _():
        lo[...] = a
        lp[...] = b

    @pl.when(step > 0)
    def _():
        lo[...] += a
        lp[...] += b

    @pl.when(step == pl.num_programs(0) - 1)
    def _():
        own, par = lo[...], lp[...]
        peak = jnp.maximum(
            jnp.max(own, axis=0, keepdims=True), jnp.max(par, axis=0, keepdims=True)
        )
        total = jnp.sum(jnp.exp(own - peak), axis=0, keepdims=True) + jnp.sum(
            jnp.exp(par - peak), axis=0, keepdims=True
        )
        cross = jnp.sum(own * to[...], axis=0, keepdims=True) + jnp.sum(
            par * tp[...], axis=0, keepdims=True
        )
        stats[...] = jnp.concatenate([peak, total, cross, jnp.zeros((5, TOK), f32)], axis=0)


def logits_of(place, blocks, passed, wo, wp, to, tp):
    steps = 2
    k = D // steps
    fixed = lambda shape: pl.BlockSpec(shape, lambda i: (0, 0))
    return pl.pallas_call(
        logits_kernel,
        grid=(steps,),
        out_shape=(
            jax.ShapeDtypeStruct((COLS, TOK), f32),
            jax.ShapeDtypeStruct((COLS, TOK), f32),
            jax.ShapeDtypeStruct((8, TOK), f32),
            jax.ShapeDtypeStruct((TOK + NY * CAP, D), bf16),
        ),
        in_specs=[pl.BlockSpec(memory_space=pltpu.SMEM)]
        + [pl.BlockSpec((b.shape[0], k), lambda i: (0, i)) for b in blocks]
        + [fixed((NY * CAP, 4 * TOPK))]
        + [pl.BlockSpec((COLS, k), lambda i: (0, i))] * 2
        + [fixed((COLS, TOK))] * 2,
        out_specs=(
            fixed((COLS, TOK)),
            fixed((COLS, TOK)),
            fixed((8, TOK)),
            pl.BlockSpec((TOK + NY * CAP, k), lambda i: (0, i)),
        ),
        compiler_params=params(),
        cost_estimate=cost(2 * TOK * D * COLS * 2, 14_000_000),
        name="logits",
    )(place, *blocks, passed, wo, wp, to, tp)


def merge(parts):
    peak = parts[0][0:1]
    for p in parts[1:]:
        peak = jnp.maximum(peak, p[0:1])
    total = sum(p[1:2] * jnp.exp(p[0:1] - peak) for p in parts)
    cross = sum(p[2:3] for p in parts)
    return peak, total, cross


def merge_kernel(shifts, *refs):
    parts = []
    for ref, shift in zip(refs[:-1], shifts):
        part = ref[...]
        if shift:
            part = pltpu.roll(part, TOK - shift * ROWS, 1)
        parts.append(part)
    peak, total, cross = merge(parts)
    refs[-1][...] = jnp.concatenate([peak, total, cross, jnp.zeros((5, TOK), f32)], axis=0)


def merged(parts, shifts):
    return pl.pallas_call(
        functools.partial(merge_kernel, shifts),
        out_shape=jax.ShapeDtypeStruct((8, TOK), f32),
        in_specs=[whole()] * len(parts),
        out_specs=whole(),
        compiler_params=params(),
        name="merge",
    )(*parts)


def row_block(peak, total, cross):
    return jnp.concatenate([peak, total, cross, jnp.zeros((5, TOK), f32)], axis=0)


def ring_kernel(before, here, after, three, two):
    b, h, a = before[...], here[...], after[...]
    three[...] = row_block(*merge([b, h, a]))
    two[...] = row_block(*merge([h, a]))


def ring_merged(before, here, after):
    return pl.pallas_call(
        ring_kernel,
        out_shape=[jax.ShapeDtypeStruct((8, TOK), f32)] * 2,
        in_specs=[whole()] * 3,
        out_specs=[whole()] * 2,
        compiler_params=params(),
        name="ring_merge",
    )(before, here, after)


def final_kernel(tk, *refs):
    peak, total, cross = merge([ref[...] for ref in refs[:-1]])
    norm = peak + jnp.log(total)
    refs[-1][...] = jnp.concatenate(
        [norm, tk[...] + norm - cross, jnp.zeros((6, TOK), f32)], axis=0
    )


def final_norm(tk, parts):
    return pl.pallas_call(
        final_kernel,
        out_shape=jax.ShapeDtypeStruct((8, TOK), f32),
        in_specs=[whole()] * (len(parts) + 1),
        out_specs=whole(),
        compiler_params=params(),
        name="norm",
    )(tk, *parts)


def gradient_kernel(lo, lp, to, tp, norm, go, gp, g_own, g_par):
    n = norm[0:1, :]
    own = (loss_scale * (jnp.exp(lo[...] - n) - to[...])).astype(bf16)
    par = (loss_scale * (jnp.exp(lp[...] - n) - tp[...])).astype(bf16)
    go[...] = own
    gp[...] = par
    g_own[...] = own.T
    g_par[...] = par.T


def gradient_of(lo, lp, to, tp, norm):
    return pl.pallas_call(
        gradient_kernel,
        out_shape=[jax.ShapeDtypeStruct((COLS, TOK), bf16)] * 2
        + [jax.ShapeDtypeStruct((TOK, COLS), bf16)] * 2,
        in_specs=[whole()] * 5,
        out_specs=[whole()] * 4,
        compiler_params=params(),
        cost_estimate=cost(0, 4_000_000),
        name="gradient",
    )(lo, lp, to, tp, norm)


def terms_kernel(place, g_own, g_par, wo, wp, *rest):
    outs_a, outs_b = rest[0:4], rest[4:8]
    x = place[0]

    def features(ref, e):
        return jnp.concatenate(
            [
                ref[:, pl.ds(pl.multiple_of((e * NX + ((x + d) & (NX - 1))) * 128, 128), 128)]
                for d in range(NX)
            ],
            axis=1,
        )

    for e in range(ZSTEP):
        out = jnp.dot(g_own[...], features(wo, e), preferred_element_type=f32)
        out = out + jnp.dot(g_par[...], features(wp, e), preferred_element_type=f32)
        at = slice(e * 128, (e + 1) * 128)
        for d in range(NX):
            for r in range(NY):
                piece = out[r * ROWS : (r + 1) * ROWS, d * 128 : (d + 1) * 128]
                outs_a[d][r, :, at] = piece[:HALF].astype(outs_a[d].dtype)
                outs_b[r][d, :, at] = piece[HALF:].astype(outs_b[r].dtype)


def terms_of(place, g_own, g_par, wo, wp):
    wide = pl.BlockSpec((COLS, ZSTEP * NX * 128), lambda e, place: (0, e))
    piece = pl.BlockSpec((4, HALF, ZSTEP * 128), lambda e, place: (0, 0, e))
    out = [jax.ShapeDtypeStruct((4, HALF, NZ * 128), t) for t in (f32, bf16, bf16, bf16)]
    return pl.pallas_call(
        terms_kernel,
        grid_spec=pltpu.PrefetchScalarGridSpec(
            num_scalar_prefetch=1,
            grid=(NZ // ZSTEP,),
            in_specs=[pl.BlockSpec((TOK, COLS), lambda e, place: (0, 0))] * 2 + [wide, wide],
            out_specs=[piece] * 8,
        ),
        out_shape=out + out,
        compiler_params=params(),
        cost_estimate=cost(2 * TOK * D * COLS * 2, 16_000_000),
        name="terms",
    )(place, g_own, g_par, wo, wp)


def sum_first_kernel(*refs):
    for half in range(2):
        ins, outs = refs[4 * half : 4 * half + 4], refs[8 + 4 * half : 12 + 4 * half]
        for r in range(4):
            total = ins[0][r]
            for ref in ins[1:]:
                total = total + ref[r].astype(f32)
            outs[r][...] = total


def sum_first(a, b):
    out = jax.ShapeDtypeStruct((HALF, NZ * 128), f32)
    res = pl.pallas_call(
        sum_first_kernel,
        out_shape=[out] * 8,
        in_specs=[whole()] * 8,
        out_specs=[whole()] * 8,
        compiler_params=params(),
        name="sum_first",
    )(*a, *b)
    return res[:4], res[4:]


def sum_second_kernel(place, *refs):
    ins_a, ins_b, outs = refs[0:4], refs[4:8], refs[8:]
    spots = ((0, 0), (1, 0), (3, 0), (3, 1), (3, 2), (4, 0), (4, 1), (2, 0))
    for e in range(NZ):
        at = pl.ds(pl.multiple_of(((place[0] + e) & (NZ - 1)) * 128, 128), 128)
        k, i = spots[e]
        outs[k][i, :HALF] = ins_a[0][:, at] + ins_a[1][:, at] + ins_a[2][:, at] + ins_a[3][:, at]
        outs[k][i, HALF:] = ins_b[0][:, at] + ins_b[1][:, at] + ins_b[2][:, at] + ins_b[3][:, at]


def sum_second(place, a, b):
    return pl.pallas_call(
        sum_second_kernel,
        out_shape=[jax.ShapeDtypeStruct((n, ROWS, 128), f32) for n in (1, 1, 1, 3, 2)],
        in_specs=[pl.BlockSpec(memory_space=pltpu.SMEM)] + [whole()] * 8,
        out_specs=[whole()] * 5,
        compiler_params=params(),
        name="sum_second",
    )(place, *a, *b)


def sum_third_kernel(own, ahead, behind, three, two, out_own, out_ahead, out_behind):
    out_own[...] = own[...] + three[1:2] + two[0:1]
    out_ahead[...] = ahead[...] + three[2:3] + two[1:2]
    out_behind[...] = behind[...] + three[0:1]


def sum_third(*values):
    return pl.pallas_call(
        sum_third_kernel,
        out_shape=[jax.ShapeDtypeStruct((1, ROWS, 128), f32)] * 3,
        in_specs=[whole()] * 5,
        out_specs=[whole()] * 3,
        compiler_params=params(),
        name="sum_third",
    )(*values)


def head_kernel(g0, g1, h0, h1, out):
    total = jnp.dot(g0[...], h0[...], preferred_element_type=f32)
    total = total + jnp.dot(g1[...], h1[...], preferred_element_type=f32)
    out[...] = total.astype(bf16)


def head_grad(g0, g1, h0, h1):
    width = 1024
    return pl.pallas_call(
        head_kernel,
        grid=(D // width,),
        out_shape=jax.ShapeDtypeStruct((COLS, D), bf16),
        in_specs=[pl.BlockSpec((COLS, TOK), lambda i: (0, 0))] * 2
        + [pl.BlockSpec((TOK, width), lambda i: (0, i))] * 2,
        out_specs=pl.BlockSpec((COLS, width), lambda i: (0, i)),
        compiler_params=params(),
        cost_estimate=cost(4 * TOK * D * COLS, 10_000_000),
        name="head_grad",
    )(g0, g1, h0, h1)


def tied(*values):
    return lax.optimization_barrier(values)


def body(hidden, head_weight, teacher_ids, teacher_logits, labels, store_ids, store_logits, owner):
    y, c, z, x = (lax.axis_index(name).astype(jnp.int32) for name in AXES)
    start = jnp.stack([index_of(y, c, z, x) * COLS, index_of(y, c + 1, z, x) * COLS])
    w_own = jnp.transpose(head_weight)

    packs = packs_of(
        jnp.stack([y, c]), owner[:, 0], teacher_ids, teacher_logits, labels[None, :], store_ids, store_logits
    )
    half = lax.dynamic_slice_in_dim(hidden, (x % 2) * HALF, HALF, 0)
    direct = send(half, dy=2)
    packs = [send(p, dy=d) if d else p for d, p in enumerate(packs)]
    *packs, direct, nearby = tied(*packs, direct, hidden)
    swapped = swap_x(direct)
    blocks = [hidden, send(nearby, dy=1), direct, swapped, send(nearby, dy=3)]
    w_par = send(w_own, dc=1)
    to, tp, tk, kept, passed = target_of(start, packs)
    lo, lp, stats, hid = logits_of(jnp.stack([x % 2, x % 2]), blocks, passed, w_own, w_par, to, tp)

    parts = [stats] + [send(stats, dx=d) for d in range(1, NX)]
    stats = merged(parts, (0,) * NX)
    parts = [stats] + [send(stats, dy=-d) for d in range(1, NY)]
    stats = merged(parts, tuple(range(NY)))
    hid_par = send(hid, dc=1)
    three, two = ring_merged(send(stats, dz=1), stats, send(stats, dz=-1))
    norm = final_norm(tk, [three, send(three, dz=-3), send(two, dz=3)])
    norm, hid_par = tied(norm, hid_par)
    next_ids, next_logits = unpacked(jnp.stack([c, y]), kept, hid_par)
    token_loss = norm[1, :ROWS]

    go, gp, g_own, g_par = gradient_of(lo, lp, to, tp, norm)
    g_other = send(gp, dc=1)
    terms = list(terms_of(jnp.stack([x, z]), g_own, g_par, w_own, w_par))
    terms[1], g_other = tied(terms[1], g_other)
    a, b = terms[0:4], terms[4:8]
    a = [a[0]] + [send(a[d], dx=d) for d in range(1, NX)]
    b = [b[0]] + [send(b[d], dy=-d) for d in range(1, NY)]
    grad_head = head_grad(go, g_other, hid, hid_par)
    *received, grad_head, next_ids, next_logits = tied(
        *a[1:], *b[1:], grad_head, next_ids, next_logits
    )
    a, b = sum_first([a[0]] + received[0:3], [b[0]] + received[3:6])
    grad_head = jnp.transpose(grad_head)
    a = [a[0]] + [send(a[d], dy=-d) for d in range(1, NY)]
    b = [b[0]] + [send(b[d], dx=d) for d in range(1, NX)]
    own, ahead, behind, three, two = sum_second(jnp.stack([z, x]), a, b)
    own, ahead, behind = sum_third(own, ahead, behind, send(three, dz=3), send(two, dz=-3))
    grad_hidden = own + send(ahead, dz=1) + send(behind, dz=-1)
    grad_hidden = grad_hidden.reshape(ROWS, 128).astype(bf16)
    return (grad_head, grad_hidden, token_loss, next_ids, next_logits)


def solution(mesh):
    fine = jax.sharding.Mesh(mesh.devices.reshape(NY, NC, NZ, NX), AXES)
    dp, vocab, both = ("y", "c"), ("z", "x"), AXES
    return jax.shard_map(
        body,
        mesh=fine,
        in_specs=(
            P(dp, None),
            P(None, both),
            P(dp, None),
            P(dp, None),
            P(dp),
            P(both, None),
            P(both, None),
            P(both, None),
        ),
        out_specs=(
            P(None, both),
            P(dp, vocab),
            P(dp),
            P(both, None),
            P(both, None),
        ),
        check_vma=False,
    )
```
